256 devices in a mesh: dev: 16 (over y, z_lo, core), ha: 16 (over x, z_hi).
Axes of the slice: x: 4, y: 4, z: 8 (z_hi: 4, z_lo: 2; z = z_hi * 2 + z_lo), core: 2. Of those that a mesh axis runs over, the one named last changes fastest.
Arguments:
- image: bfloat16 [32, 64, 256, 256], P(None, 'dev', 'ha'), may hold values from -6 to 6
- kernel_one: bfloat16 [64, 32, 3, 3, 3], replicated, may hold values from -0.21875 to 0.21875
- kernel_two: bfloat16 [128, 64, 3, 3, 3], P('ha'), may hold values from -0.15625 to 0.15625
- cotangent: bfloat16 [128, 16, 64, 64], P('ha', 'dev'), may hold values from -6 to 6
Outputs:
- activation: bfloat16 [128, 16, 64, 64], P('ha', 'dev')
- grad_pooled: bfloat16 [64, 16, 64, 64], P(None, 'dev', 'ha')
- grad_one: float32 [64, 32, 3, 3, 3], replicated
- grad_two: float32 [128, 64, 3, 3, 3], P('ha')
The draws below stay inside these ranges and needn't reach their ends.
All inputs are finite; a program needn't handle non-finite values.
Results may differ from the reference program's by a relative error of at most 0.02.
Values may be sent and summed in bfloat16 or wider, within the bound.
No kernel may reach another device: no remote copies, remote signals or barrier semaphores. Data moves between devices by JAX's collectives and lax.ppermute only.
A program may use at most 128 MiB of HBM per device.

```python
import math
import jax
import jax.numpy as jnp
from jax import lax

CH_IN = 32
CH_MID = 64
CH_OUT = 128
WIDE = 256
DEPTH = 64
HEIGHT = 256
CELLS_ONE = 524288
CELLS_TWO = 65536


def levels(rng, shape, split, low, top_value):
    def one(position, parts):
        draws = jax.random.uniform(jax.random.fold_in(jax.random.fold_in(rng, 6), position), (parts,), jnp.float32, low / len(split), top_value / len(split))
        return jnp.repeat(jnp.exp(draws), shape[position] // parts).reshape((-1,) + (1,) * (len(shape) - position - 1))

    factor_of = one(*split[0])
    for cut in split[1:]:
        factor_of = factor_of * one(*cut)
    return factor_of


def normal_values(own_key, shape, spread, bound, cuts=(), held_as=jnp.bfloat16):
    array = jax.random.normal(own_key, shape, jnp.float32) * spread
    if len(cuts) > 0:
        array = levels(own_key, shape, cuts, -0.22, 0.18) * array
    return jnp.clip(array, min=-bound, max=bound).astype(held_as)


def setup_inputs(seed: int = 0) -> dict:
    keys = jax.random.split(jax.random.key(seed), 5)
    image = normal_values(keys[0], (CH_IN, DEPTH, HEIGHT, WIDE), 1.0, 6.0, ((1, 16), (2, 16)))
    kernel_one = normal_values(keys[1], (CH_MID, CH_IN, 3, 3, 3), (CH_IN * 27) ** -0.5, 0.21875)
    kernel_two = normal_values(keys[2], (CH_OUT, CH_MID, 3, 3, 3), (CH_MID * 27) ** -0.5, 0.15625, ((0, 16),))
    cotangent = normal_values(keys[3], (CH_OUT, DEPTH // 4, HEIGHT // 4, WIDE // 4), 1.0, 6.0, ((0, 16), (1, 16)))
    return {"image": image, "kernel_one": kernel_one, "kernel_two": kernel_two, "cotangent": cotangent}


def convolve(field, kernel, strides):
    return lax.conv_general_dilated(field[None], kernel, strides, 'VALID', dimension_numbers=('NCDHW', 'OIDHW', 'NCDHW'), preferred_element_type=jnp.float32)[0]

def filter_grad(field, deltas, dilation):
    result = lax.conv_general_dilated(field[None], deltas[None], (1, 1, 1), 'VALID', rhs_dilation=(dilation, dilation, dilation), dimension_numbers=('CNDHW', 'IODHW', 'NCDHW'), preferred_element_type=jnp.float32)
    return jnp.transpose(result, (1, 0, 2, 3, 4))

def average_pool(field):
    chans, depth, height, width = field.shape
    return field.reshape(chans, depth // 2, 2, height // 2, 2, width // 2, 2).mean(axis=(2, 4, 6))

def expand_pool(field):
    chans, depth, height, width = field.shape
    grown = jnp.broadcast_to(field[:, :, None, :, None, :, None], (chans, depth, 2, height, 2, width, 2))
    return grown.reshape(chans, 2 * depth, 2 * height, 2 * width)

def silu_slope(value):
    sigma = jax.nn.sigmoid(value)
    return sigma * (1.0 + value * (1.0 - sigma))

def reference(image, kernel_one, kernel_two, cotangent):
    padded = jnp.pad(image, ((0, 0), (1, 0), (1, 0), (1, 0)))
    pre_one = convolve(padded, kernel_one, (2, 2, 2))
    pooled = average_pool(jax.nn.silu(pre_one)).astype(jnp.bfloat16)
    pooled_pad = jnp.pad(pooled, ((0, 0), (1, 1), (1, 1), (1, 1)))
    pre_two = convolve(pooled_pad, kernel_two, (1, 1, 1))
    activation = jax.nn.silu(pre_two).astype(jnp.bfloat16)
    delta_two = (cotangent.astype(jnp.float32) * silu_slope(pre_two)).astype(jnp.bfloat16)
    grad_two = filter_grad(pooled_pad, delta_two, 1) / math.sqrt(CELLS_TWO)
    flipped = jnp.transpose(jnp.flip(kernel_two, (2, 3, 4)), (1, 0, 2, 3, 4))
    delta_pad = jnp.pad(delta_two, ((0, 0), (1, 1), (1, 1), (1, 1)))
    back_pooled = convolve(delta_pad, flipped, (1, 1, 1))
    grad_pooled = back_pooled.astype(jnp.bfloat16)
    delta_one = (expand_pool(back_pooled) * 0.125 * silu_slope(pre_one)).astype(jnp.bfloat16)
    grad_one = filter_grad(padded, delta_one, 2) * (8.0 / math.sqrt(CELLS_ONE))
    return (activation, grad_pooled, grad_one, grad_two)
```

```python
import math

import jax
import jax.numpy as jnp
from jax import lax
from jax.experimental import pallas as pl
from jax.experimental.pallas import tpu as pltpu
from jax.sharding import PartitionSpec as P

BF = jnp.bfloat16
F32 = jnp.float32
CELLS_ONE = 524288
CELLS_TWO = 65536
VMEM_LIMIT = 32 * 1024 * 1024


def call(body, out_shape, args, scratch=(), flops=1000000):
    moved = sum(math.prod(s.shape) * s.dtype.itemsize for s in list(out_shape) + list(args))
    return pl.pallas_call(
        body,
        out_shape=out_shape,
        in_specs=[pl.BlockSpec(memory_space=pltpu.VMEM)] * len(args),
        out_specs=[pl.BlockSpec(memory_space=pltpu.VMEM)] * len(out_shape),
        scratch_shapes=scratch,
        compiler_params=pltpu.CompilerParams(vmem_limit_bytes=VMEM_LIMIT),
        cost_estimate=pl.CostEstimate(flops=flops, bytes_accessed=moved, transcendentals=0),
    )(*args)


def shape(dims, dtype):
    return jax.ShapeDtypeStruct(dims, dtype)


def lanes(dims):
    return lax.broadcasted_iota(jnp.int32, dims, len(dims) - 1)


def rows_of(dims):
    return lax.broadcasted_iota(jnp.int32, dims, len(dims) - 2)


def mm(a, b):
    return lax.dot_general(a, b, (((1,), (0,)), ((), ())), preferred_element_type=F32)


def mm_nt(a, b):
    return lax.dot_general(a, b, (((1,), (1,)), ((), ())), preferred_element_type=F32)


def split_mm(a, sel, terms):
    total = None
    for _ in range(terms):
        part = a.astype(BF)
        a = a - part.astype(F32)
        term = mm(part, sel)
        total = term if total is None else total + term
    return total


def pack_filters_body(k_ref, cot_ref, out_ref, acc, cots):
    pieces = []
    for pair in range(14):
        left = k_ref[2 * pair].astype(F32)
        right = k_ref[2 * pair + 1].astype(F32) if pair < 13 else jnp.zeros((8, 64), F32)
        pieces.append(jnp.concatenate([left, right], axis=1))
    filters = jnp.concatenate(pieces, axis=1)
    for h in range(16):
        acc[8 * h : 8 * h + 8, 0:1792] = filters
    cots[...] = jnp.concatenate([cot_ref[...].astype(F32), jnp.zeros((512, 64), F32)], axis=1)
    for h in range(16):
        for half in range(2):
            row = 4 * h + 2 * half
            first = cots[pl.ds(row, 8, stride=64), :]
            second = cots[pl.ds(row + 1, 8, stride=64), :]
            acc[8 * h : 8 * h + 8, 1792 + 128 * half : 1920 + 128 * half] = first + pltpu.roll(second, 64, 1)
    out_ref[...] = acc[...].astype(BF)


def first_layer_body(x_ref, plane_ref, row_ref, corner_ref, w_ref, xt_ref, slope_ref, pooled_ref, top_ref, bot_ref, ev, od):
    w_in, n_out = rows_of((256, 256)), lanes((256, 256))
    sel = (w_in == jnp.where(n_out < 128, 2 * n_out, 2 * n_out - 255)).astype(F32).astype(BF)

    def spread(value, at):
        both = mm(value, sel)
        ev[at : at + value.shape[0], :] = both[:, :128]
        od[at : at + value.shape[0], :] = both[:, 128:]

    for part in range(8):
        spread(x_ref[256 * part : 256 * part + 256, :], 256 * part)
    for part in range(2):
        spread(plane_ref[256 * part : 256 * part + 256, :], 2048 + 256 * part)
    spread(row_ref[...], 2560)
    spread(corner_ref[...], 2688)

    first_lane = lanes((32, 128)) == 0
    for a in range(5):
        for b in range(17):
            if a > 0:
                start, stride = ((a - 1) * 16 + b - 1, 64) if b > 0 else (2560 + a - 1, 4)
            else:
                start, stride = (2048 + b - 1, 16) if b > 0 else (2688, 1)
            even = ev[pl.ds(start, 32, stride=stride), :]
            odd = od[pl.ds(start, 32, stride=stride), :]
            before = jnp.where(first_lane, 0.0, pltpu.roll(odd, 1, 1))
            xt_ref[a * 17 + b, 0:32, :] = before.astype(BF)
            xt_ref[a * 17 + b, 32:64, :] = even.astype(BF)
            xt_ref[a * 17 + b, 64:96, :] = odd.astype(BF)

    weights = jnp.transpose(w_ref[...].astype(F32), (1, 0)).astype(BF)
    sums = [None] * 4
    for i in range(2):
        for jp in range(4):
            pre = mm(weights, patches_one(xt_ref, i, jp))
            sigma = jax.nn.sigmoid(pre)
            at = (i * 4 + jp) * 256
            slope_ref[:, at : at + 256] = sigma * (1.0 + pre * (1.0 - sigma)) * 0.125
            act = pre * sigma
            both = act[:, :128] + act[:, 128:]
            sums[jp] = both if i == 0 else sums[jp] + both
    k_in, k_out = rows_of((256, 128)), lanes((256, 128))
    fold = ((k_in // 2) == k_out).astype(F32).astype(BF)
    halves = []
    for pair in range(2):
        stacked = jnp.concatenate([sums[2 * pair], sums[2 * pair + 1]], axis=1)
        halves.append(split_mm(stacked, fold, 3) * 0.125)
    pooled = jnp.concatenate(halves, axis=1)
    pooled_ref[...] = pooled.astype(BF)
    top_ref[...] = pooled[:, 0:64].astype(BF)
    bot_ref[...] = pltpu.roll(pooled, 64, 1)[:, 0:64].astype(BF)


def patches_one(xt_ref, i, jp):
    columns = []
    for j in (2 * jp, 2 * jp + 1):
        blocks = [xt_ref[(2 * i + a) * 17 + 2 * j + b] for a in range(3) for b in range(3)]
        columns.append(jnp.concatenate(blocks, axis=0))
    return jnp.concatenate(columns, axis=1)


def shifted(ext):
    dims = ext.shape
    column = lanes(dims) & 63
    for e in range(3):
        if e == 0:
            moved = jnp.where(column == 0, 0.0, pltpu.roll(ext, 1, 1))
        elif e == 2:
            moved = jnp.where(column == 63, 0.0, pltpu.roll(ext, 383, 1))
        else:
            moved = ext
        yield (0, e), moved[:, 0:256]
        yield (1, e), pltpu.roll(moved, 320, 1)[:, 0:256]
        yield (2, e), moved[:, 128:384]


def second_layer_body(before_ref, own_ref, after_ref, a2_ref, patches_ref, act_ref, delta_ref, top_ref, bot_ref):
    for a, ref in enumerate((before_ref, own_ref, after_ref)):
        for (b, e), value in shifted(ref[...].astype(F32)):
            t = a * 9 + b * 3 + e
            patches_ref[64 * t : 64 * t + 64, :] = value.astype(BF)
    patches_ref[1728:1792, :] = jnp.zeros((64, 256), BF)
    pre = mm(a2_ref[:, 0:1792], patches_ref[...])
    sigma = jax.nn.sigmoid(pre)
    act_ref[...] = (pre * sigma).astype(BF)
    slope = sigma * (1.0 + pre * (1.0 - sigma))
    delta = a2_ref[:, 1792:2048].astype(F32) * slope
    delta_ref[...] = delta.astype(BF)
    top_ref[...] = delta[:, 0:64].astype(BF)
    bot_ref[...] = pltpu.roll(delta, 64, 1)[:, 0:64].astype(BF)


def grad_two_body(delta_ref, patches_ref, out_ref):
    r, o = rows_of((128, 128)), lanes((128, 128))
    order = (o == (r % 16) * 8 + r // 16).astype(F32).astype(BF)
    delta = mm(order, delta_ref[...]).astype(BF)
    grad = mm_nt(delta, patches_ref[...]).astype(BF)
    for q in range(8):
        for half in range(2):
            d = 2 * q + half
            out_ref[16 * d : 16 * d + 16, :] = grad[16 * q : 16 * q + 16, 896 * half : 896 * half + 896]


def turn_filters_body(a2_ref, out_ref):
    for pair in range(14):
        block = a2_ref[:, 128 * pair : 128 * pair + 128].astype(F32)
        turned = jnp.transpose(block, (1, 0)).astype(BF)
        out_ref[:, 256 * pair : 256 * pair + 128] = turned[0:64, :]
        if pair < 13:
            out_ref[:, 256 * pair + 128 : 256 * pair + 256] = turned[64:128, :]


def backward_body(before_ref, own_ref, after_ref, wb_ref, slope_ref, xt_ref, g2_ref, pooled_ref, out_ref, pd, one):
    for a, ref in enumerate((before_ref, own_ref, after_ref)):
        for (b, e), value in shifted(ref[...].astype(F32)):
            t = 26 - (a * 9 + b * 3 + e)
            pd[128 * t : 128 * t + 128, :] = value.astype(BF)
    back = mm(wb_ref[...], pd[...])
    for r in range(4):
        turned = back if r == 0 else pltpu.roll(back, 256 - 64 * r, 1)
        pooled_ref[:, r, :] = turned[:, 0:64].astype(BF)
    w_in, n_out = rows_of((128, 256)), lanes((128, 256))
    total = jnp.zeros((64, 1024), F32)
    grown = []
    for pair in range(2):
        grow = (w_in == n_out // 2).astype(F32).astype(BF)
        grown.append(split_mm(back[:, 128 * pair : 128 * pair + 128], grow, 3))
    for i in range(2):
        for jp in range(4):
            row = grown[jp // 2][:, 128 * (jp % 2) : 128 * (jp % 2) + 128]
            at = (i * 4 + jp) * 256
            delta = (jnp.concatenate([row, row], axis=1) * slope_ref[:, at : at + 256]).astype(BF)
            cells = patches_one(xt_ref, i, jp)
            blank = jnp.zeros((32, 256), BF)
            chunks = []
            for s in range(4):
                chunks += [cells[224 * s : min(224 * s + 224, 864), :], blank]
            chunks.append(blank)
            total = total + mm_nt(delta, jnp.concatenate(chunks, axis=0))
    for s in range(4):
        for quarter in range(4):
            for side in range(2):
                at = 256 * s + 128 * side
                one[side, pl.ds(s * 4 + quarter, 16, stride=16), :] = total[16 * quarter : 16 * quarter + 16, at : at + 128]
    out_ref[:, 0:896] = g2_ref[...]
    out_ref[:, 896:1024] = one[0].astype(BF)
    out_ref[:, 1024:1152] = one[1].astype(BF)


def sum_depth_body(in_ref, act_ref, out_ref, acc):
    total = in_ref[0:16, :].astype(F32)
    for d in range(1, 16):
        total = total + in_ref[16 * d : 16 * d + 16, :].astype(F32)
    act = act_ref[...].astype(F32)
    acc[...] = jnp.zeros(acc.shape, F32)
    for side in range(2):
        for m in range(4):
            at = 256 * m + 128 * side
            if at < 896:
                acc[side, pl.ds(8 + m, 16, stride=16), :] = total[:, at : at + 128]
        for h in range(16):
            acc[side, 16 * h : 16 * h + 8, :] = act[8 * h : 8 * h + 8, 128 * side : 128 * side + 128]
        out_ref[:, 256 + 128 * side : 384 + 128 * side] = acc[side].astype(BF)
    one = total[:, 896:1152].astype(BF)
    for h in range(16):
        out_ref[16 * h : 16 * h + 16, 0:256] = one


def sum_height_body(in_ref, act_ref, out_ref, acc):
    total = in_ref[0:16, :].astype(F32)
    for h in range(16):
        block = in_ref[16 * h : 16 * h + 16, :].astype(F32)
        if h > 0:
            total = total + block
        for r in range(4):
            side, odd = r // 2, r % 2
            value = block[0:8, 256 + 128 * side : 384 + 128 * side]
            acc[pl.ds(4 * h + r, 8, stride=64), :] = pltpu.roll(value, 64, 1) if odd else value
    act_ref[...] = acc[...][:, 0:64].astype(BF)
    for d in range(16):
        out_ref[24 * d : 24 * d + 16, :] = total[:, 0:256]
        out_ref[24 * d + 16 : 24 * d + 24, :] = total[8:16, 256:512]


def finish_body(in_ref, one_ref, two_ref, acc):
    for side in range(2):
        acc[side, :, :] = in_ref[:, 128 * side : 128 * side + 128]
    for half in range(2):
        for m in range(4):
            for side in range(2):
                if 256 * m + 128 * side >= 896:
                    continue
                value = acc[side, pl.ds(24 * half + 16 + m, 8, stride=48), :] * (1.0 / math.sqrt(CELLS_TWO))
                t = 14 * half + 4 * m + 2 * side
                two_ref[t] = value[:, 0:64]
                if t + 1 < 27:
                    two_ref[t + 1] = pltpu.roll(value, 64, 1)[:, 0:64]
    scale = 8.0 / math.sqrt(CELLS_ONE)
    for s in range(4):
        for side in range(2):
            rows = [acc[side, pl.ds(s * 4 + quarter, 16, stride=24), :] for quarter in range(4)]
            turned = jnp.transpose(jnp.concatenate(rows, axis=0), (1, 0)) * scale
            for k in range(4):
                t = 7 * s + 4 * side + k
                if 4 * side + k < 7 and t < 27:
                    one_ref[t] = turned[32 * k : 32 * k + 32, :]


def move(block, axis, step):
    size = lax.axis_size(axis)
    return lax.ppermute(block, axis, [(i, i + step) for i in range(size) if 0 <= i + step < size])


def exchange(block, axis):
    return lax.all_to_all(block, axis, 0, 0, tiled=True)


def with_rims(own, top, bot):
    wide = jnp.concatenate([move(bot, "ha", 1), own, move(top, "ha", -1)], axis=1)
    return move(wide, "dev", 1), wide, move(wide, "dev", -1)


def shards(image, kernel_one, kernel_two, cotangent):
    n_dev, n_ha = lax.axis_size("dev"), lax.axis_size("ha")
    x = image.reshape(2048, 256)
    plane = move(image[:, 3].reshape(512, 256), "dev", 1)
    row = move(image[:, :, 15].reshape(128, 256), "ha", 1)
    corner = lax.ppermute(
        image[:, 3, 15],
        ("dev", "ha"),
        [(d * n_ha + h, (d + 1) * n_ha + h + 1) for d in range(n_dev - 1) for h in range(n_ha - 1)],
    )
    k1 = jnp.transpose(kernel_one, (2, 3, 4, 1, 0)).reshape(864, 64)
    k2 = jnp.transpose(kernel_two, (2, 3, 4, 0, 1)).reshape(27, 8, 64)
    cot = cotangent.reshape(512, 64)
    (packed,) = call(
        pack_filters_body,
        [shape((128, 2048), BF)],
        [k2, cot],
        [pltpu.VMEM((128, 2048), F32), pltpu.VMEM((512, 128), F32)],
    )
    a2 = exchange(packed, "ha")
    xt, slope, pooled, top, bot = call(
        first_layer_body,
        [shape((85, 96, 128), BF), shape((64, 2048), F32), shape((64, 256), BF), shape((64, 64), BF), shape((64, 64), BF)],
        [x, plane, row, corner, k1],
        [pltpu.VMEM((2720, 128), F32), pltpu.VMEM((2720, 128), F32)],
        flops=500000000,
    )
    (wb,) = call(turn_filters_body, [shape((64, 3456), BF)], [a2])
    before, own, after = with_rims(pooled, top, bot)
    patches, act, delta, dtop, dbot = call(
        second_layer_body,
        [shape((1792, 256), BF), shape((128, 256), BF), shape((128, 256), BF), shape((128, 64), BF), shape((128, 64), BF)],
        [before, own, after, a2],
        flops=120000000,
    )
    (g2,) = call(grad_two_body, [shape((256, 896), BF)], [delta, patches], flops=120000000)
    dbefore, down, dafter = with_rims(delta, dtop, dbot)
    grad_pooled, payload = call(
        backward_body,
        [shape((64, 4, 64), BF), shape((256, 1152), BF)],
        [dbefore, down, dafter, wb, slope, xt, g2],
        [pltpu.VMEM((3456, 256), BF), pltpu.VMEM((2, 256, 128), F32)],
        flops=400000000,
    )
    (second,) = call(
        sum_depth_body, [shape((256, 512), BF)], [exchange(payload, "dev"), act], [pltpu.VMEM((2, 256, 128), F32)]
    )
    activation, third = call(
        sum_height_body,
        [shape((512, 64), BF), shape((384, 256), F32)],
        [exchange(second, "ha")],
        [pltpu.VMEM((512, 128), F32)],
    )
    one, two = call(
        finish_body,
        [shape((27, 32, 64), F32), shape((27, 8, 64), F32)],
        [exchange(third, "dev")],
        [pltpu.VMEM((2, 384, 128), F32)],
    )
    grad_one = jnp.transpose(one.reshape(3, 3, 3, 32, 64), (4, 3, 0, 1, 2))
    grad_two = jnp.transpose(two.reshape(3, 3, 3, 8, 64), (3, 4, 0, 1, 2))
    return (activation.reshape(8, 1, 64, 64), grad_pooled.reshape(64, 1, 4, 64), grad_one, grad_two)


def solution(mesh):
    return jax.shard_map(
        shards,
        mesh=mesh,
        in_specs=(
            P(None, "dev", "ha", None),
            P(),
            P("ha", None, None, None, None),
            P("ha", "dev", None, None),
        ),
        out_specs=(
            P("ha", "dev", None, None),
            P(None, "dev", "ha", None),
            P(),
            P("ha", None, None, None, None),
        ),
        check_vma=False,
    )
```

```python
import math

import jax
import jax.numpy as jnp
from jax import lax
from jax.experimental import pallas as pl
from jax.experimental.pallas import tpu as pltpu
from jax.sharding import PartitionSpec as P

BF = jnp.bfloat16
F32 = jnp.float32
CELLS_ONE = 524288
CELLS_TWO = 65536
VMEM_LIMIT = 32 * 1024 * 1024


def call(body, out_shape, args, scratch=(), flops=1000000):
    moved = sum(math.prod(s.shape) * s.dtype.itemsize for s in list(out_shape) + list(args))
    return pl.pallas_call(
        body,
        out_shape=out_shape,
        in_specs=[pl.BlockSpec(memory_space=pltpu.VMEM)] * len(args),
        out_specs=[pl.BlockSpec(memory_space=pltpu.VMEM)] * len(out_shape),
        scratch_shapes=scratch,
        compiler_params=pltpu.CompilerParams(vmem_limit_bytes=VMEM_LIMIT),
        cost_estimate=pl.CostEstimate(flops=flops, bytes_accessed=moved, transcendentals=0),
    )(*args)


def shape(dims, dtype):
    return jax.ShapeDtypeStruct(dims, dtype)


def lanes(dims):
    return lax.broadcasted_iota(jnp.int32, dims, len(dims) - 1)


def rows_of(dims):
    return lax.broadcasted_iota(jnp.int32, dims, len(dims) - 2)


def mm(a, b):
    return lax.dot_general(a, b, (((1,), (0,)), ((), ())), preferred_element_type=F32)


def mm_nt(a, b):
    return lax.dot_general(a, b, (((1,), (1,)), ((), ())), preferred_element_type=F32)


def split_mm(a, sel, terms):
    total = None
    for _ in range(terms):
        part = a.astype(BF)
        a = a - part.astype(F32)
        term = mm(part, sel)
        total = term if total is None else total + term
    return total


def pack_body(x_ref, k_ref, cot_ref, plane_ref, row_ref, corner_ref, out_ref, last, acc, cots):
    for c in range(32):
        plane_ref[16 * c : 16 * c + 16, :] = x_ref[64 * c + 48 : 64 * c + 64, :]
    for part in range(128):
        block = x_ref[16 * part : 16 * part + 16, :].astype(F32)[8:16]
        for side in range(2):
            last[side, 8 * part : 8 * part + 8, :] = block[:, 128 * side : 128 * side + 128]
    for side in range(2):
        at = 128 * side
        row_ref[:, at : at + 128] = last[side, pl.ds(7, 128, stride=8), :].astype(BF)
        corner_ref[:, at : at + 128] = last[side, pl.ds(31, 32, stride=32), :].astype(BF)
    pieces = []
    for pair in range(14):
        left = k_ref[2 * pair].astype(F32)
        right = k_ref[2 * pair + 1].astype(F32) if pair < 13 else jnp.zeros((8, 64), F32)
        pieces.append(jnp.concatenate([left, right], axis=1))
    filters = jnp.concatenate(pieces, axis=1)
    for h in range(16):
        acc[8 * h : 8 * h + 8, 0:1792] = filters
    cots[...] = jnp.concatenate([cot_ref[...].astype(F32), jnp.zeros((512, 64), F32)], axis=1)
    for h in range(16):
        for part in range(3):
            two = []
            for row in (4 * h - 1 + 2 * part, 4 * h + 2 * part):
                two.append(cots[pl.ds(row, 8, stride=64), :] if 0 <= row < 64 else jnp.zeros((8, 128), F32))
            at = 1792 + 128 * part
            acc[8 * h : 8 * h + 8, at : at + 128] = two[0] + pltpu.roll(two[1], 64, 1)
    out_ref[...] = acc[...].astype(BF)


def first_layer_body(x_ref, plane_ref, row_ref, corner_ref, w_ref, xt_ref, slope_ref, pooled_ref, one_ref, other_ref, ev, od):
    w_in, n_out = rows_of((256, 256)), lanes((256, 256))
    sel = (w_in == jnp.where(n_out < 128, 2 * n_out, 2 * n_out - 255)).astype(F32).astype(BF)

    def spread(value, at):
        both = mm(value, sel)
        ev[at : at + value.shape[0], :] = both[:, :128]
        od[at : at + value.shape[0], :] = both[:, 128:]

    for part in range(8):
        spread(x_ref[256 * part : 256 * part + 256, :], 256 * part)
    for part in range(2):
        spread(plane_ref[256 * part : 256 * part + 256, :], 2048 + 256 * part)
    spread(row_ref[...], 2560)
    spread(corner_ref[...], 2688)

    first_lane = lanes((32, 128)) == 0
    for a in range(5):
        for b in range(17):
            if a > 0:
                start, stride = ((a - 1) * 16 + b - 1, 64) if b > 0 else (2560 + a - 1, 4)
            else:
                start, stride = (2048 + b - 1, 16) if b > 0 else (2688, 1)
            even = ev[pl.ds(start, 32, stride=stride), :]
            odd = od[pl.ds(start, 32, stride=stride), :]
            before = jnp.where(first_lane, 0.0, pltpu.roll(odd, 1, 1))
            xt_ref[a * 17 + b, 0:32, :] = before.astype(BF)
            xt_ref[a * 17 + b, 32:64, :] = even.astype(BF)
            xt_ref[a * 17 + b, 64:96, :] = odd.astype(BF)

    weights = jnp.transpose(w_ref[...].astype(F32), (1, 0)).astype(BF)
    sums = [None] * 4
    for i in range(2):
        for jp in range(4):
            pre = mm(weights, patches_one(xt_ref, i, jp))
            sigma = jax.nn.sigmoid(pre)
            at = (i * 4 + jp) * 256
            slope_ref[:, at : at + 256] = sigma * (1.0 + pre * (1.0 - sigma)) * 0.125
            act = pre * sigma
            both = act[:, :128] + act[:, 128:]
            sums[jp] = both if i == 0 else sums[jp] + both
    k_in, k_out = rows_of((256, 128)), lanes((256, 128))
    fold = ((k_in // 2) == k_out).astype(F32).astype(BF)
    halves = []
    for pair in range(2):
        stacked = jnp.concatenate([sums[2 * pair], sums[2 * pair + 1]], axis=1)
        halves.append(split_mm(stacked, fold, 3) * 0.125)
    pooled = jnp.concatenate(halves, axis=1)
    pooled_ref[...] = pooled.astype(BF)
    even = is_even("ha")
    one_ref[...] = jnp.where(even, halves[1], halves[0]).astype(BF)
    other_ref[...] = jnp.where(even, halves[0], halves[1]).astype(BF)


def patches_one(xt_ref, i, jp):
    columns = []
    for j in (2 * jp, 2 * jp + 1):
        blocks = [xt_ref[(2 * i + a) * 17 + 2 * j + b] for a in range(3) for b in range(3)]
        columns.append(jnp.concatenate(blocks, axis=0))
    return jnp.concatenate(columns, axis=1)


def is_even(axis):
    return lax.axis_index(axis) % 2 == 0


def ordered(own_ref, core_ref, cross_ref):
    core, cross = core_ref[...].astype(F32), cross_ref[...].astype(F32)
    even = is_even("dev")
    return (jnp.where(even, cross, core), own_ref[...].astype(F32), jnp.where(even, core, cross))


def shifted(ext):
    width = ext.shape[1]
    kept = width - 128
    column = lanes(ext.shape) & 63
    for e in range(3):
        if e == 0:
            moved = jnp.where(column == 0, 0.0, pltpu.roll(ext, 1, 1))
        elif e == 2:
            moved = jnp.where(column == 63, 0.0, pltpu.roll(ext, width - 1, 1))
        else:
            moved = ext
        yield (0, e), moved[:, 0:kept]
        yield (1, e), pltpu.roll(moved, width - 64, 1)[:, 0:kept]
        yield (2, e), moved[:, 128:width]


def second_layer_body(own_ref, core_ref, cross_ref, a2_ref, patches_ref, act_ref, delta_ref):
    even = is_even("ha")
    for a, plane in enumerate(ordered(own_ref, core_ref, cross_ref)):
        one, other = plane[:, 0:128], plane[:, 384:512]
        plane = jnp.concatenate([jnp.where(even, other, one), plane[:, 128:384], jnp.where(even, one, other)], axis=1)
        for (b, e), value in shifted(plane):
            t = a * 9 + b * 3 + e
            patches_ref[64 * t : 64 * t + 64, :] = value.astype(BF)
    patches_ref[1728:1792, :] = jnp.zeros((64, 384), BF)
    pre = mm(a2_ref[:, 0:1792], patches_ref[...])
    sigma = jax.nn.sigmoid(pre)
    act_ref[...] = pltpu.roll(pre * sigma, 320, 1)[:, 0:256].astype(BF)
    slope = sigma * (1.0 + pre * (1.0 - sigma))
    delta_ref[...] = (a2_ref[:, 1792:2176].astype(F32) * slope).astype(BF)


def grad_two_body(delta_ref, patches_ref, out_ref):
    r, o = rows_of((128, 128)), lanes((128, 128))
    order = (o == (r % 16) * 8 + r // 16).astype(F32).astype(BF)
    cell = lanes((128, 384))
    mine = (cell >= 64) & (cell < 320)
    delta = jnp.where(mine, mm(order, delta_ref[...]), 0.0).astype(BF)
    grad = mm_nt(delta, patches_ref[...]).astype(BF)
    for q in range(8):
        for half in range(2):
            d = 2 * q + half
            out_ref[16 * d : 16 * d + 16, :] = grad[16 * q : 16 * q + 16, 896 * half : 896 * half + 896]


def turn_filters_body(a2_ref, out_ref):
    for pair in range(14):
        block = a2_ref[:, 128 * pair : 128 * pair + 128].astype(F32)
        turned = jnp.transpose(block, (1, 0)).astype(BF)
        out_ref[:, 256 * pair : 256 * pair + 128] = turned[0:64, :]
        if pair < 13:
            out_ref[:, 256 * pair + 128 : 256 * pair + 256] = turned[64:128, :]


def backward_body(own_ref, core_ref, cross_ref, wb_ref, slope_ref, xt_ref, g2_ref, pooled_ref, out_ref, pd, one):
    for a, plane in enumerate(ordered(own_ref, core_ref, cross_ref)):
        for (b, e), value in shifted(plane):
            t = 26 - (a * 9 + b * 3 + e)
            pd[128 * t : 128 * t + 128, :] = value.astype(BF)
    back = mm(wb_ref[...], pd[...])
    for r in range(4):
        turned = back if r == 0 else pltpu.roll(back, 256 - 64 * r, 1)
        pooled_ref[:, r, :] = turned[:, 0:64].astype(BF)
    w_in, n_out = rows_of((128, 256)), lanes((128, 256))
    total = jnp.zeros((64, 1024), F32)
    grown = []
    for pair in range(2):
        grow = (w_in == n_out // 2).astype(F32).astype(BF)
        grown.append(split_mm(back[:, 128 * pair : 128 * pair + 128], grow, 3))
    for i in range(2):
        for jp in range(4):
            row = grown[jp // 2][:, 128 * (jp % 2) : 128 * (jp % 2) + 128]
            at = (i * 4 + jp) * 256
            delta = (jnp.concatenate([row, row], axis=1) * slope_ref[:, at : at + 256]).astype(BF)
            cells = patches_one(xt_ref, i, jp)
            blank = jnp.zeros((32, 256), BF)
            chunks = []
            for s in range(4):
                chunks += [cells[224 * s : min(224 * s + 224, 864), :], blank]
            chunks.append(blank)
            total = total + mm_nt(delta, jnp.concatenate(chunks, axis=0))
    for s in range(4):
        for quarter in range(4):
            for side in range(2):
                at = 256 * s + 128 * side
                one[side, pl.ds(s * 4 + quarter, 16, stride=16), :] = total[16 * quarter : 16 * quarter + 16, at : at + 128]
    out_ref[:, 0:896] = g2_ref[...]
    out_ref[:, 896:1024] = one[0].astype(BF)
    out_ref[:, 1024:1152] = one[1].astype(BF)


def sum_depth_body(in_ref, act_ref, out_ref, acc):
    total = in_ref[0:16, :].astype(F32)
    for d in range(1, 16):
        total = total + in_ref[16 * d : 16 * d + 16, :].astype(F32)
    act = act_ref[...].astype(F32)
    acc[...] = jnp.zeros(acc.shape, F32)
    for m in range(7):
        acc[1, pl.ds(m, 16, stride=16), :] = total[:, 128 * m : 128 * m + 128]
    for h in range(16):
        for side in range(2):
            at = 16 * h + 8 * side
            acc[0, at : at + 8, :] = act[8 * h : 8 * h + 8, 128 * side : 128 * side + 128]
    out_ref[:, 256:384] = acc[0].astype(BF)
    out_ref[:, 384:512] = acc[1].astype(BF)
    one = total[:, 896:1152].astype(BF)
    for h in range(16):
        out_ref[16 * h : 16 * h + 16, 0:256] = one


def sum_height_body(in_ref, act_ref, out_ref, acc):
    one, two = None, None
    for h in range(16):
        block = in_ref[16 * h : 16 * h + 16, :].astype(F32)
        one = block[:, 0:256] if h == 0 else one + block[:, 0:256]
        two = block[:, 384:512] if h == 0 else two + block[:, 384:512]
        for r in range(4):
            value = block[8 * (r // 2) : 8 * (r // 2) + 8, 256:384]
            acc[pl.ds(4 * h + r, 8, stride=64), :] = pltpu.roll(value, 64, 1) if r % 2 else value
    act_ref[...] = acc[...][:, 0:64].astype(BF)
    packed = jnp.concatenate([one, two], axis=1).astype(BF)
    for d in range(16):
        out_ref[16 * d : 16 * d + 16, :] = packed


def finish_body(in_ref, one_ref, two_ref, acc):
    for part in range(3):
        acc[part, :, :] = in_ref[:, 128 * part : 128 * part + 128].astype(F32)
    for half in range(2):
        for m in range(7):
            value = acc[2, pl.ds(16 * half + m, 8, stride=32), :] * (1.0 / math.sqrt(CELLS_TWO))
            t = 14 * half + 2 * m
            two_ref[t] = value[:, 0:64]
            if t + 1 < 27:
                two_ref[t + 1] = pltpu.roll(value, 64, 1)[:, 0:64]
    scale = 8.0 / math.sqrt(CELLS_ONE)
    for s in range(4):
        for side in range(2):
            rows = [acc[side, pl.ds(s * 4 + quarter, 16, stride=16), :] for quarter in range(4)]
            turned = jnp.transpose(jnp.concatenate(rows, axis=0), (1, 0)) * scale
            for k in range(4):
                t = 7 * s + 4 * side + k
                if 4 * side + k < 7 and t < 27:
                    one_ref[t] = turned[32 * k : 32 * k + 32, :]


def move(block, axis, step):
    size = lax.axis_size(axis)
    return lax.ppermute(block, axis, [(i, i + step) for i in range(size) if 0 <= i + step < size])


def swap(block, axis, first):
    pairs = [(i, i + 1) for i in range(first, lax.axis_size(axis) - 1, 2)]
    return lax.ppermute(block, axis, pairs + [(j, i) for i, j in pairs])


def exchange(block, axis):
    return lax.all_to_all(block, axis, 0, 0, tiled=True)


def shards(image, kernel_one, kernel_two, cotangent):
    n_dev, n_ha = lax.axis_size("dev"), lax.axis_size("ha")
    x = image.reshape(2048, 256)
    k1 = jnp.transpose(kernel_one, (2, 3, 4, 1, 0)).reshape(864, 64)
    k2 = jnp.transpose(kernel_two, (2, 3, 4, 0, 1)).reshape(27, 8, 64)
    cot = cotangent.reshape(512, 64)
    plane, row, corner, packed = call(
        pack_body,
        [shape((512, 256), BF), shape((128, 256), BF), shape((32, 256), BF), shape((128, 2176), BF)],
        [x, k2, cot],
        [pltpu.VMEM((2, 1024, 128), F32), pltpu.VMEM((128, 2176), F32), pltpu.VMEM((512, 128), F32)],
    )
    plane = move(plane, "dev", 1)
    row = move(row, "ha", 1)
    corner = lax.ppermute(
        corner,
        ("dev", "ha"),
        [(d * n_ha + h, (d + 1) * n_ha + h + 1) for d in range(n_dev - 1) for h in range(n_ha - 1)],
    )
    plane, row, corner, packed = lax.optimization_barrier((plane, row, corner, packed))
    a2 = exchange(packed, "ha")
    xt, slope, pooled, one, other = call(
        first_layer_body,
        [shape((85, 96, 128), BF), shape((64, 2048), F32), shape((64, 256), BF), shape((64, 128), BF), shape((64, 128), BF)],
        [x, plane, row, corner, k1],
        [pltpu.VMEM((2720, 128), F32), pltpu.VMEM((2720, 128), F32)],
        flops=500000000,
    )
    (wb,) = call(turn_filters_body, [shape((64, 3456), BF)], [a2])
    wide = jnp.concatenate([swap(one, "ha", 0), pooled, swap(other, "ha", 1)], axis=1)
    patches, act, delta = call(
        second_layer_body,
        [shape((1792, 384), BF), shape((128, 256), BF), shape((128, 384), BF)],
        [wide, swap(wide, "dev", 0), swap(wide, "dev", 1), a2],
        flops=180000000,
    )
    (g2,) = call(grad_two_body, [shape((256, 896), BF)], [delta, patches], flops=180000000)
    grad_pooled, payload = call(
        backward_body,
        [shape((64, 4, 64), BF), shape((256, 1152), BF)],
        [delta, swap(delta, "dev", 0), swap(delta, "dev", 1), wb, slope, xt, g2],
        [pltpu.VMEM((3456, 256), BF), pltpu.VMEM((2, 256, 128), F32)],
        flops=400000000,
    )
    (second,) = call(
        sum_depth_body, [shape((256, 512), BF)], [exchange(payload, "dev"), act], [pltpu.VMEM((2, 256, 128), F32)]
    )
    activation, third = call(
        sum_height_body,
        [shape((512, 64), BF), shape((256, 384), BF)],
        [exchange(second, "ha")],
        [pltpu.VMEM((512, 128), F32)],
    )
    one, two = call(
        finish_body,
        [shape((27, 32, 64), F32), shape((27, 8, 64), F32)],
        [exchange(third, "dev")],
        [pltpu.VMEM((3, 256, 128), F32)],
    )
    grad_one = jnp.transpose(one.reshape(3, 3, 3, 32, 64), (4, 3, 0, 1, 2))
    grad_two = jnp.transpose(two.reshape(3, 3, 3, 8, 64), (3, 4, 0, 1, 2))
    return (activation.reshape(8, 1, 64, 64), grad_pooled.reshape(64, 1, 4, 64), grad_one, grad_two)


def solution(mesh):
    return jax.shard_map(
        shards,
        mesh=mesh,
        in_specs=(
            P(None, "dev", "ha", None),
            P(),
            P("ha", None, None, None, None),
            P("ha", "dev", None, None),
        ),
        out_specs=(
            P("ha", "dev", None, None),
            P(None, "dev", "ha", None),
            P(),
            P("ha", None, None, None, None),
        ),
        check_vma=False,
    )
```

```python
import math

import jax
import jax.numpy as jnp
from jax import lax
from jax.experimental import pallas as pl
from jax.experimental.pallas import tpu as pltpu
from jax.sharding import PartitionSpec as P

BF = jnp.bfloat16
F32 = jnp.float32
CELLS_ONE = 524288
CELLS_TWO = 65536
VMEM_LIMIT = 32 * 1024 * 1024


def call(body, out_shape, args, scratch=(), flops=1000000):
    moved = sum(math.prod(s.shape) * s.dtype.itemsize for s in list(out_shape) + list(args))
    return pl.pallas_call(
        body,
        out_shape=out_shape,
        in_specs=[pl.BlockSpec(memory_space=pltpu.VMEM)] * len(args),
        out_specs=[pl.BlockSpec(memory_space=pltpu.VMEM)] * len(out_shape),
        scratch_shapes=scratch,
        compiler_params=pltpu.CompilerParams(vmem_limit_bytes=VMEM_LIMIT),
        cost_estimate=pl.CostEstimate(flops=flops, bytes_accessed=moved, transcendentals=0),
    )(*args)


def shape(dims, dtype):
    return jax.ShapeDtypeStruct(dims, dtype)


def lanes(dims):
    return lax.broadcasted_iota(jnp.int32, dims, len(dims) - 1)


def rows_of(dims):
    return lax.broadcasted_iota(jnp.int32, dims, len(dims) - 2)


def mm(a, b):
    return lax.dot_general(a, b, (((1,), (0,)), ((), ())), preferred_element_type=F32)


def mm_nt(a, b):
    return lax.dot_general(a, b, (((1,), (1,)), ((), ())), preferred_element_type=F32)


def split_mm(a, sel, terms):
    total = None
    for _ in range(terms):
        part = a.astype(BF)
        a = a - part.astype(F32)
        term = mm(part, sel)
        total = term if total is None else total + term
    return total


def edges_body(x_ref, plane_ref, row_ref, corner_ref, last):
    for c in range(32):
        plane_ref[16 * c : 16 * c + 16, :] = x_ref[64 * c + 48 : 64 * c + 64, :]
    for part in range(128):
        block = x_ref[16 * part : 16 * part + 16, :].astype(F32)[8:16]
        for side in range(2):
            last[side, 8 * part : 8 * part + 8, :] = block[:, 128 * side : 128 * side + 128]
    for side in range(2):
        row_ref[:, 128 * side : 128 * side + 128] = last[side, pl.ds(7, 128, stride=8), :].astype(BF)
        corner_ref[:, 128 * side : 128 * side + 128] = last[side, pl.ds(31, 32, stride=32), :].astype(BF)


def pack_body(k_ref, cot_ref, _, out_ref, acc, cots):
    even = is_even("dev")
    pieces = []
    for pair in range(7):
        taps = []
        for t in (2 * pair, 2 * pair + 1):
            high = k_ref[t + 14].astype(F32) if t < 13 else jnp.zeros((8, 64), F32)
            taps.append(jnp.where(even, k_ref[t].astype(F32), high))
        pieces.append(jnp.concatenate(taps, axis=1))
    filters = jnp.concatenate(pieces, axis=1)
    for h in range(16):
        acc[8 * h : 8 * h + 8, 0:896] = filters
    cots[...] = jnp.concatenate([cot_ref[...].astype(F32), jnp.zeros((512, 64), F32)], axis=1)
    for h in range(16):
        for part in range(3):
            two = []
            for row in (4 * h - 1 + 2 * part, 4 * h + 2 * part):
                two.append(cots[pl.ds(row, 8, stride=64), :] if 0 <= row < 64 else jnp.zeros((8, 128), F32))
            at = 896 + 128 * part
            acc[8 * h : 8 * h + 8, at : at + 128] = two[0] + pltpu.roll(two[1], 64, 1)
    out_ref[...] = acc[...].astype(BF)


def parted(value, ev, od, at):
    w_in, n_out = rows_of((256, 256)), lanes((256, 256))
    sel = (w_in == jnp.where(n_out < 128, 2 * n_out, 2 * n_out - 255)).astype(F32).astype(BF)
    both = mm(value, sel)
    ev[at : at + value.shape[0], :] = both[:, :128]
    od[at : at + value.shape[0], :] = both[:, 128:]


def place(out_ref, index, ev, od, start, stride):
    even = ev[pl.ds(start, 32, stride=stride), :]
    odd = od[pl.ds(start, 32, stride=stride), :]
    before = jnp.where(lanes((32, 128)) == 0, 0.0, pltpu.roll(odd, 1, 1))
    out_ref[index, 0:32, :] = before.astype(BF)
    out_ref[index, 32:64, :] = even.astype(BF)
    out_ref[index, 64:96, :] = odd.astype(BF)


def turn_image_body(x_ref, w_ref, own_ref, wt_ref, ev, od):
    for part in range(8):
        parted(x_ref[256 * part : 256 * part + 256, :], ev, od, 256 * part)
    for row in range(64):
        place(own_ref, row, ev, od, row, 64)
    wt_ref[...] = jnp.transpose(w_ref[...].astype(F32), (1, 0)).astype(BF)


def first_layer_body(own_ref, wt_ref, plane_ref, row_ref, corner_ref, slope_ref, pooled_ref, one_ref, other_ref, low_ref, top_ref, ev, od):
    for part in range(2):
        parted(plane_ref[256 * part : 256 * part + 256, :], ev, od, 256 * part)
    parted(row_ref[...], ev, od, 512)
    parted(corner_ref[...], ev, od, 640)
    for r in range(16):
        place(low_ref, r, ev, od, r, 16)
    place(top_ref, 0, ev, od, 640, 1)
    for p in range(4):
        place(top_ref, 1 + p, ev, od, 512 + p, 4)
    weights = wt_ref[...]
    sums = [None] * 4
    for i in range(2):
        for jp in range(4):
            pre = mm(weights, patches_one(own_ref, low_ref, top_ref, i, jp))
            sigma = jax.nn.sigmoid(pre)
            at = (i * 4 + jp) * 256
            slope_ref[:, at : at + 256] = sigma * (1.0 + pre * (1.0 - sigma)) * 0.125
            act = pre * sigma
            both = act[:, :128] + act[:, 128:]
            sums[jp] = both if i == 0 else sums[jp] + both
    k_in, k_out = rows_of((256, 128)), lanes((256, 128))
    fold = ((k_in // 2) == k_out).astype(F32).astype(BF)
    halves = []
    for pair in range(2):
        stacked = jnp.concatenate([sums[2 * pair], sums[2 * pair + 1]], axis=1)
        halves.append(split_mm(stacked, fold, 3) * 0.125)
    pooled = jnp.concatenate(halves, axis=1)
    pooled_ref[...] = pooled.astype(BF)
    even = is_even("ha")
    one_ref[...] = jnp.where(even, halves[1], halves[0]).astype(BF)
    other_ref[...] = jnp.where(even, halves[0], halves[1]).astype(BF)


def patches_one(own_ref, low_ref, top_ref, i, jp):
    def block(a, b):
        if b == 0:
            return top_ref[a]
        return low_ref[b - 1] if a == 0 else own_ref[(a - 1) * 16 + b - 1]

    columns = []
    for j in (2 * jp, 2 * jp + 1):
        columns.append(jnp.concatenate([block(2 * i + a, 2 * j + b) for a in range(3) for b in range(3)], axis=0))
    return jnp.concatenate(columns, axis=1)


def is_even(axis):
    return lax.axis_index(axis) % 2 == 0


def ordered(own_ref, core_ref, cross_ref):
    core, cross = core_ref[...].astype(F32), cross_ref[...].astype(F32)
    even = is_even("dev")
    return (jnp.where(even, cross, core), own_ref[...].astype(F32), jnp.where(even, core, cross))


def shifted(ext):
    width = ext.shape[1]
    kept = width - 128
    column = lanes(ext.shape) & 63
    for e in range(3):
        if e == 0:
            moved = jnp.where(column == 0, 0.0, pltpu.roll(ext, 1, 1))
        elif e == 2:
            moved = jnp.where(column == 63, 0.0, pltpu.roll(ext, width - 1, 1))
        else:
            moved = ext
        yield (0, e), moved[:, 0:kept]
        yield (1, e), pltpu.roll(moved, width - 64, 1)[:, 0:kept]
        yield (2, e), moved[:, 128:width]


def second_layer_body(own_ref, core_ref, cross_ref, w2_ref, a2_ref, patches_ref, act_ref, delta_ref):
    even = is_even("ha")
    for a, plane in enumerate(ordered(own_ref, core_ref, cross_ref)):
        one, other = plane[:, 0:128], plane[:, 384:512]
        plane = jnp.concatenate([jnp.where(even, other, one), plane[:, 128:384], jnp.where(even, one, other)], axis=1)
        for (b, e), value in shifted(plane):
            t = a * 9 + b * 3 + e
            patches_ref[64 * t : 64 * t + 64, :] = value.astype(BF)
    patches_ref[1728:1792, :] = jnp.zeros((64, 384), BF)
    pre = mm(w2_ref[...], patches_ref[...])
    sigma = jax.nn.sigmoid(pre)
    act_ref[...] = pltpu.roll(pre * sigma, 320, 1)[:, 0:256].astype(BF)
    slope = sigma * (1.0 + pre * (1.0 - sigma))
    delta_ref[...] = (a2_ref[:, 896:1280].astype(F32) * slope).astype(BF)


def grad_two_body(delta_ref, patches_ref, keep_ref, give_ref):
    r, o = rows_of((128, 128)), lanes((128, 128))
    order = (o == (r % 16) * 8 + r // 16).astype(F32).astype(BF)
    cell = lanes((128, 384))
    mine = (cell >= 64) & (cell < 320)
    delta = jnp.where(mine, mm(order, delta_ref[...]), 0.0).astype(BF)
    grad = mm_nt(delta, patches_ref[...])
    even = is_even("dev")
    keep_ref[...] = jnp.where(even, grad[:, 0:896], grad[:, 896:1792])
    give_ref[...] = jnp.where(even, grad[:, 896:1792], grad[:, 0:896]).astype(BF)


def turn_filters_body(mine_ref, other_ref, w2_ref, wb_ref):
    even = is_even("dev")
    for pair in range(14):
        at = 128 * (pair % 7)
        mine, other = mine_ref[:, at : at + 128].astype(F32), other_ref[:, at : at + 128].astype(F32)
        block = jnp.where(even, mine, other) if pair < 7 else jnp.where(even, other, mine)
        w2_ref[:, 128 * pair : 128 * pair + 128] = block.astype(BF)
        turned = jnp.transpose(block, (1, 0)).astype(BF)
        wb_ref[:, 256 * pair : 256 * pair + 128] = turned[0:64, :]
        if pair < 13:
            wb_ref[:, 256 * pair + 128 : 256 * pair + 256] = turned[64:128, :]


def backward_body(own_ref, core_ref, cross_ref, wb_ref, slope_ref, image_ref, low_ref, rim_ref, pooled_ref, keep_ref, give_ref, pd, one):
    for a, plane in enumerate(ordered(own_ref, core_ref, cross_ref)):
        for (b, e), value in shifted(plane):
            t = 26 - (a * 9 + b * 3 + e)
            pd[128 * t : 128 * t + 128, :] = value.astype(BF)
    back = mm(wb_ref[...], pd[...])
    for r in range(4):
        turned = back if r == 0 else pltpu.roll(back, 256 - 64 * r, 1)
        pooled_ref[:, r, :] = turned[:, 0:64].astype(BF)
    w_in, n_out = rows_of((128, 256)), lanes((128, 256))
    total = jnp.zeros((64, 1024), F32)
    grown = []
    for pair in range(2):
        grow = (w_in == n_out // 2).astype(F32).astype(BF)
        grown.append(split_mm(back[:, 128 * pair : 128 * pair + 128], grow, 3))
    for i in range(2):
        for jp in range(4):
            row = grown[jp // 2][:, 128 * (jp % 2) : 128 * (jp % 2) + 128]
            at = (i * 4 + jp) * 256
            delta = (jnp.concatenate([row, row], axis=1) * slope_ref[:, at : at + 256]).astype(BF)
            cells = patches_one(image_ref, low_ref, rim_ref, i, jp)
            blank = jnp.zeros((32, 256), BF)
            chunks = []
            for s in range(4):
                chunks += [cells[224 * s : min(224 * s + 224, 864), :], blank]
            chunks.append(blank)
            total = total + mm_nt(delta, jnp.concatenate(chunks, axis=0))
    for s in range(4):
        for quarter in range(4):
            for side in range(2):
                at = 256 * s + 128 * side
                one[side, pl.ds(s * 4 + quarter, 16, stride=16), :] = total[16 * quarter : 16 * quarter + 16, at : at + 128]
    even = is_even("dev")
    for c in range(8):
        for side in range(2):
            at = 128 * side
            first, second = one[side, 32 * c : 32 * c + 16, :], one[side, 32 * c + 16 : 32 * c + 32, :]
            keep_ref[16 * c : 16 * c + 16, at : at + 128] = jnp.where(even, first, second)
            give_ref[16 * c : 16 * c + 16, at : at + 128] = jnp.where(even, second, first).astype(BF)


def sum_chip_body(two_ref, other_two_ref, one_ref, other_one_ref, out_ref):
    out_ref[:, 0:896] = (two_ref[...] + other_two_ref[...].astype(F32)).astype(BF)
    out_ref[:, 896:1152] = (one_ref[...] + other_one_ref[...].astype(F32)).astype(BF)


def sum_depth_body(in_ref, act_ref, out_ref, acc):
    total = in_ref[0:16, :].astype(F32)
    for d in range(1, 8):
        total = total + in_ref[16 * d : 16 * d + 16, :].astype(F32)
    act = act_ref[...].astype(F32)
    acc[...] = jnp.zeros(acc.shape, F32)
    for m in range(7):
        acc[1, pl.ds(m, 16, stride=16), :] = total[:, 128 * m : 128 * m + 128]
    for h in range(16):
        for side in range(2):
            at = 16 * h + 8 * side
            acc[0, at : at + 8, :] = act[8 * h : 8 * h + 8, 128 * side : 128 * side + 128]
    out_ref[:, 256:384] = acc[0].astype(BF)
    out_ref[:, 384:512] = acc[1].astype(BF)
    one = total[:, 896:1152].astype(BF)
    for h in range(16):
        out_ref[16 * h : 16 * h + 16, 0:256] = one


def sum_height_body(in_ref, act_ref, out_ref, acc):
    one, two = None, None
    for h in range(16):
        block = in_ref[16 * h : 16 * h + 16, :].astype(F32)
        one = block[:, 0:256] if h == 0 else one + block[:, 0:256]
        two = block[:, 384:512] if h == 0 else two + block[:, 384:512]
        for r in range(4):
            value = block[8 * (r // 2) : 8 * (r // 2) + 8, 256:384]
            acc[pl.ds(4 * h + r, 8, stride=64), :] = pltpu.roll(value, 64, 1) if r % 2 else value
    act_ref[...] = acc[...][:, 0:64].astype(BF)
    packed = jnp.concatenate([one, two], axis=1).astype(BF)
    for d in range(16):
        out_ref[16 * d : 16 * d + 16, :] = packed


def finish_body(in_ref, one_ref, two_ref, acc):
    for part in range(3):
        acc[part, :, :] = in_ref[:, 128 * part : 128 * part + 128].astype(F32)
    for half in range(2):
        for m in range(7):
            value = acc[2, pl.ds(16 * half + m, 8, stride=32), :] * (1.0 / math.sqrt(CELLS_TWO))
            t = 14 * half + 2 * m
            two_ref[t] = value[:, 0:64]
            if t + 1 < 27:
                two_ref[t + 1] = pltpu.roll(value, 64, 1)[:, 0:64]
    scale = 8.0 / math.sqrt(CELLS_ONE)
    for s in range(4):
        for side in range(2):
            rows = [acc[side, pl.ds(s * 4 + quarter, 16, stride=16), :] for quarter in range(4)]
            turned = jnp.transpose(jnp.concatenate(rows, axis=0), (1, 0)) * scale
            for k in range(4):
                t = 7 * s + 4 * side + k
                if 4 * side + k < 7 and t < 27:
                    one_ref[t] = turned[32 * k : 32 * k + 32, :]


def move(block, axis, step):
    size = lax.axis_size(axis)
    return lax.ppermute(block, axis, [(i, i + step) for i in range(size) if 0 <= i + step < size])


def swap(block, axis, first):
    pairs = [(i, i + 1) for i in range(first, lax.axis_size(axis) - 1, 2)]
    return lax.ppermute(block, axis, pairs + [(j, i) for i, j in pairs])


def exchange(block, axis, groups=None):
    return lax.all_to_all(block, axis, 0, 0, tiled=True, axis_index_groups=groups)


def shards(image, kernel_one, kernel_two, cotangent):
    x = image.reshape(2048, 256)
    k1 = jnp.transpose(kernel_one, (2, 3, 4, 1, 0)).reshape(864, 64)
    k2 = jnp.transpose(kernel_two, (2, 3, 4, 0, 1)).reshape(27, 8, 64)
    cot = cotangent.reshape(512, 64)
    plane, row, corner = call(
        edges_body,
        [shape((512, 256), BF), shape((128, 256), BF), shape((32, 256), BF)],
        [x],
        [pltpu.VMEM((2, 1024, 128), F32)],
    )
    (packed,) = call(
        pack_body,
        [shape((128, 1280), BF)],
        [k2, cot, row],
        [pltpu.VMEM((128, 1280), F32), pltpu.VMEM((512, 128), F32)],
    )
    plane = move(plane, "dev", 1)
    row = move(row, "ha", 1)
    n_dev, n_ha = lax.axis_size("dev"), lax.axis_size("ha")
    corner = lax.ppermute(
        corner,
        ("dev", "ha"),
        [(d * n_ha + h, (d + 1) * n_ha + h + 1) for d in range(n_dev - 1) for h in range(n_ha - 1)],
    )
    a2 = exchange(packed, "ha")
    own, wt = call(
        turn_image_body,
        [shape((64, 96, 128), BF), shape((64, 864), BF)],
        [x, k1],
        [pltpu.VMEM((2048, 128), F32), pltpu.VMEM((2048, 128), F32)],
        flops=300000000,
    )
    slope, pooled, one, other, low, top = call(
        first_layer_body,
        [
            shape((64, 2048), F32),
            shape((64, 256), BF),
            shape((64, 128), BF),
            shape((64, 128), BF),
            shape((16, 96, 128), BF),
            shape((5, 96, 128), BF),
        ],
        [own, wt, plane, row, corner],
        [pltpu.VMEM((672, 128), F32), pltpu.VMEM((672, 128), F32)],
        flops=400000000,
    )
    w2, wb = call(turn_filters_body, [shape((128, 1792), BF), shape((64, 3456), BF)], [a2, swap(a2, "dev", 0)])
    wide = jnp.concatenate([swap(one, "ha", 0), pooled, swap(other, "ha", 1)], axis=1)
    patches, act, delta = call(
        second_layer_body,
        [shape((1792, 384), BF), shape((128, 256), BF), shape((128, 384), BF)],
        [wide, swap(wide, "dev", 0), swap(wide, "dev", 1), w2, a2],
        flops=180000000,
    )
    keep_two, give_two = call(
        grad_two_body, [shape((128, 896), F32), shape((128, 896), BF)], [delta, patches], flops=180000000
    )
    grad_pooled, keep_one, give_one = call(
        backward_body,
        [shape((64, 4, 64), BF), shape((128, 256), F32), shape((128, 256), BF)],
        [delta, swap(delta, "dev", 0), swap(delta, "dev", 1), wb, slope, own, low, top],
        [pltpu.VMEM((3456, 256), BF), pltpu.VMEM((2, 256, 128), F32)],
        flops=400000000,
    )
    (first,) = call(
        sum_chip_body,
        [shape((128, 1152), BF)],
        [keep_two, swap(give_two, "dev", 0), keep_one, swap(give_one, "dev", 0)],
    )
    same_core = [list(range(core, lax.axis_size("dev"), 2)) for core in range(2)]
    (second,) = call(
        sum_depth_body,
        [shape((256, 512), BF)],
        [exchange(first, "dev", same_core), act],
        [pltpu.VMEM((2, 256, 128), F32)],
    )
    activation, third = call(
        sum_height_body,
        [shape((512, 64), BF), shape((256, 384), BF)],
        [exchange(second, "ha")],
        [pltpu.VMEM((512, 128), F32)],
    )
    one, two = call(
        finish_body,
        [shape((27, 32, 64), F32), shape((27, 8, 64), F32)],
        [exchange(third, "dev")],
        [pltpu.VMEM((3, 256, 128), F32)],
    )
    grad_one = jnp.transpose(one.reshape(3, 3, 3, 32, 64), (4, 3, 0, 1, 2))
    grad_two = jnp.transpose(two.reshape(3, 3, 3, 8, 64), (3, 4, 0, 1, 2))
    return (activation.reshape(8, 1, 64, 64), grad_pooled.reshape(64, 1, 4, 64), grad_one, grad_two)


def solution(mesh):
    return jax.shard_map(
        shards,
        mesh=mesh,
        in_specs=(
            P(None, "dev", "ha", None),
            P(),
            P("ha", None, None, None, None),
            P("ha", "dev", None, None),
        ),
        out_specs=(
            P("ha", "dev", None, None),
            P(None, "dev", "ha", None),
            P(),
            P("ha", None, None, None, None),
        ),
        check_vma=False,
    )
```

```python
import math

import jax
import jax.numpy as jnp
from jax import lax
from jax.experimental import pallas as pl
from jax.experimental.pallas import tpu as pltpu
from jax.sharding import PartitionSpec as P

BF = jnp.bfloat16
F32 = jnp.float32
CELLS_ONE = 524288
CELLS_TWO = 65536
VMEM_LIMIT = 32 * 1024 * 1024


def call(body, out_shape, args, scratch=(), flops=1000000, space=pltpu.VMEM, limit=VMEM_LIMIT):
    moved = sum(math.prod(s.shape) * s.dtype.itemsize for s in list(out_shape) + list(args))
    return pl.pallas_call(
        body,
        out_shape=out_shape,
        in_specs=[pl.BlockSpec(memory_space=space)] * len(args),
        out_specs=[pl.BlockSpec(memory_space=pltpu.VMEM)] * len(out_shape),
        scratch_shapes=scratch,
        compiler_params=pltpu.CompilerParams(vmem_limit_bytes=limit),
        cost_estimate=pl.CostEstimate(flops=flops, bytes_accessed=moved, transcendentals=0),
    )(*args)


def shape(dims, dtype):
    return jax.ShapeDtypeStruct(dims, dtype)


def lanes(dims):
    return lax.broadcasted_iota(jnp.int32, dims, len(dims) - 1)


def rows_of(dims):
    return lax.broadcasted_iota(jnp.int32, dims, len(dims) - 2)


def mm(a, b):
    return lax.dot_general(a, b, (((1,), (0,)), ((), ())), preferred_element_type=F32)


def mm_nt(a, b):
    return lax.dot_general(a, b, (((1,), (1,)), ((), ())), preferred_element_type=F32)


def split_mm(a, sel, terms):
    total = None
    for _ in range(terms):
        part = a.astype(BF)
        a = a - part.astype(F32)
        term = mm(part, sel)
        total = term if total is None else total + term
    return total


def pack_body(x_hbm, k_hbm, cot_hbm, plane_ref, row_ref, corner_ref, out_ref, x_ref, k_ref, cot_ref, last, acc, cots, sems):
    copies = []
    for i, (src, dst) in enumerate([(x_hbm, x_ref), (k_hbm, k_ref), (cot_hbm, cot_ref)]):
        copies.append(pltpu.make_async_copy(src, dst, sems.at[i]))
        copies[i].start()
    copies[1].wait()
    even = is_even("dev")
    pieces = []
    for pair in range(7):
        taps = []
        for t in (2 * pair, 2 * pair + 1):
            high = k_ref[t + 14].astype(F32) if t < 13 else jnp.zeros((8, 64), F32)
            taps.append(jnp.where(even, k_ref[t].astype(F32), high))
        pieces.append(jnp.concatenate(taps, axis=1))
    filters = jnp.concatenate(pieces, axis=1)
    for h in range(16):
        acc[8 * h : 8 * h + 8, 0:896] = filters
    copies[2].wait()
    cots[...] = jnp.concatenate([cot_ref[...].astype(F32), jnp.zeros((512, 64), F32)], axis=1)
    for h in range(16):
        for part in range(3):
            two = []
            for row in (4 * h - 1 + 2 * part, 4 * h + 2 * part):
                two.append(cots[pl.ds(row, 8, stride=64), :] if 0 <= row < 64 else jnp.zeros((8, 128), F32))
            at = 896 + 128 * part
            acc[8 * h : 8 * h + 8, at : at + 128] = two[0] + pltpu.roll(two[1], 64, 1)
    out_ref[...] = acc[...].astype(BF)
    copies[0].wait()
    for c in range(32):
        plane_ref[16 * c : 16 * c + 16, :] = x_ref[64 * c + 48 : 64 * c + 64, :]
    for part in range(128):
        block = x_ref[16 * part : 16 * part + 16, :].astype(F32)[8:16]
        for side in range(2):
            last[side, 8 * part : 8 * part + 8, :] = block[:, 128 * side : 128 * side + 128]
    for side in range(2):
        at = 128 * side
        row_ref[:, at : at + 128] = last[side, pl.ds(7, 128, stride=8), :].astype(BF)
        corner_ref[:, at : at + 128] = last[side, pl.ds(31, 32, stride=32), :].astype(BF)


def parted(value, ev, od, at):
    w_in, n_out = rows_of((256, 256)), lanes((256, 256))
    sel = (w_in == jnp.where(n_out < 128, 2 * n_out, 2 * n_out - 255)).astype(F32).astype(BF)
    both = mm(value, sel)
    ev[at : at + value.shape[0], :] = both[:, :128]
    od[at : at + value.shape[0], :] = both[:, 128:]


def place(out_ref, index, ev, od, start, stride):
    even = ev[pl.ds(start, 32, stride=stride), :]
    odd = od[pl.ds(start, 32, stride=stride), :]
    before = jnp.where(lanes((32, 128)) == 0, 0.0, pltpu.roll(odd, 1, 1))
    out_ref[index, 0:32, :] = before.astype(BF)
    out_ref[index, 32:64, :] = even.astype(BF)
    out_ref[index, 64:96, :] = odd.astype(BF)


def turn_image_body(x_ref, w_ref, own_ref, wt_ref, ev, od):
    for part in range(8):
        parted(x_ref[256 * part : 256 * part + 256, :], ev, od, 256 * part)
    for row in range(64):
        place(own_ref, row, ev, od, row, 64)
    wt_ref[...] = jnp.transpose(w_ref[...].astype(F32), (1, 0)).astype(BF)


def first_layer_body(own_ref, wt_ref, plane_ref, row_ref, corner_ref, slope_ref, pooled_ref, low_ref, top_ref, ev, od):
    for part in range(2):
        parted(plane_ref[256 * part : 256 * part + 256, :], ev, od, 256 * part)
    parted(row_ref[...], ev, od, 512)
    parted(corner_ref[...], ev, od, 640)
    for r in range(16):
        place(low_ref, r, ev, od, r, 16)
    place(top_ref, 0, ev, od, 640, 1)
    for p in range(4):
        place(top_ref, 1 + p, ev, od, 512 + p, 4)
    weights = wt_ref[...]
    sums = [None] * 4
    for i in range(2):
        for jp in range(4):
            pre = mm(weights, patches_one(own_ref, low_ref, top_ref, i, jp))
            sigma = jax.nn.sigmoid(pre)
            at = (i * 4 + jp) * 256
            slope_ref[:, at : at + 256] = sigma * (1.0 + pre * (1.0 - sigma)) * 0.125
            act = pre * sigma
            both = act[:, :128] + act[:, 128:]
            sums[jp] = both if i == 0 else sums[jp] + both
    k_in, k_out = rows_of((256, 128)), lanes((256, 128))
    fold = ((k_in // 2) == k_out).astype(F32).astype(BF)
    halves = []
    for pair in range(2):
        stacked = jnp.concatenate([sums[2 * pair], sums[2 * pair + 1]], axis=1)
        halves.append(split_mm(stacked, fold, 3) * 0.125)
    pooled = jnp.concatenate(halves, axis=1)
    pooled_ref[...] = pooled.astype(BF)


def patches_one(own_ref, low_ref, top_ref, i, jp):
    def block(a, b):
        if b == 0:
            return top_ref[a]
        return low_ref[b - 1] if a == 0 else own_ref[(a - 1) * 16 + b - 1]

    columns = []
    for j in (2 * jp, 2 * jp + 1):
        columns.append(jnp.concatenate([block(2 * i + a, 2 * j + b) for a in range(3) for b in range(3)], axis=0))
    return jnp.concatenate(columns, axis=1)


def is_even(axis):
    return lax.axis_index(axis) % 2 == 0


def shifted(ext):
    width = ext.shape[1]
    kept = width - 128
    column = lanes(ext.shape) & 63
    for e in range(3):
        if e == 0:
            moved = jnp.where(column == 0, 0.0, pltpu.roll(ext, 1, 1))
        elif e == 2:
            moved = jnp.where(column == 63, 0.0, pltpu.roll(ext, width - 1, 1))
        else:
            moved = ext
        yield (0, e), moved[:, 0:kept]
        yield (1, e), pltpu.roll(moved, width - 64, 1)[:, 0:kept]
        yield (2, e), moved[:, 128:width]


def rims_body(own_ref, other_ref, out_ref):
    bottom = is_even("ha") == is_even("dev")
    for k, ref in enumerate((own_ref, other_ref)):
        value = ref[...].astype(F32)
        out_ref[64 * k : 64 * k + 64, :] = jnp.where(bottom, value[:, 128:256], value[:, 0:128]).astype(BF)


def widen_body(own_ref, other_ref, mine_ref, core_ref, a2_ref, out_ref):
    swapped = is_even("ha") == is_even("dev")
    mine, core = mine_ref[...].astype(F32), core_ref[...].astype(F32)
    for k, ref in enumerate((own_ref, other_ref)):
        here, there = mine[64 * k : 64 * k + 64], core[64 - 64 * k : 128 - 64 * k]
        out_ref[64 * k : 64 * k + 64, 0:128] = jnp.where(swapped, there, here).astype(BF)
        out_ref[64 * k : 64 * k + 64, 128:384] = ref[...]
        out_ref[64 * k : 64 * k + 64, 384:512] = jnp.where(swapped, here, there).astype(BF)
    out_ref[:, 512:896] = a2_ref[:, 896:1280]


def second_layer_body(pair_ref, cross_ref, core_ref, w2_ref, other_ref, patches_ref, act_ref, delta_ref):
    even = is_even("dev")

    def planes(ref):
        return ref[0:64, 0:512].astype(F32), ref[64:128, 0:512].astype(F32)

    own, other = planes(pair_ref)
    near, far = planes(cross_ref)
    beyond = core_ref[0:64, 0:512].astype(F32)
    ordered = (
        jnp.where(even, far, beyond),
        jnp.where(even, near, other),
        own,
        jnp.where(even, other, near),
        jnp.where(even, beyond, far),
    )
    for a, plane in enumerate(ordered):
        for (b, e), value in shifted(plane):
            t = a * 9 + b * 3 + e
            patches_ref[64 * t : 64 * t + 64, :] = value.astype(BF)
    patches_ref[2880:2944, :] = jnp.zeros((64, 384), BF)
    cot_cross, cot_core = cross_ref[:, 512:896].astype(F32), other_ref[:, 896:1280].astype(F32)
    cots = (
        jnp.where(even, cot_cross, cot_core),
        pair_ref[:, 512:896].astype(F32),
        jnp.where(even, cot_core, cot_cross),
    )
    for p in range(3):
        pre = mm(w2_ref[...], patches_ref[576 * p : 576 * p + 1792, :])
        sigma = jax.nn.sigmoid(pre)
        if p == 1:
            act_ref[...] = pltpu.roll(pre * sigma, 320, 1)[:, 0:256].astype(BF)
        slope = sigma * (1.0 + pre * (1.0 - sigma))
        delta_ref[128 * p : 128 * p + 128, :] = (cots[p] * slope).astype(BF)


def grad_two_body(delta_ref, patches_ref, keep_ref, give_ref):
    r, o = rows_of((128, 128)), lanes((128, 128))
    order = (o == (r % 16) * 8 + r // 16).astype(F32).astype(BF)
    cell = lanes((128, 384))
    mine = (cell >= 64) & (cell < 320)
    delta = jnp.where(mine, mm(order, delta_ref[128:256, :]), 0.0).astype(BF)
    grad = mm_nt(delta, patches_ref[576:2368, :])
    even = is_even("dev")
    keep_ref[...] = jnp.where(even, grad[:, 0:896], grad[:, 896:1792])
    give_ref[...] = jnp.where(even, grad[:, 896:1792], grad[:, 0:896]).astype(BF)


def turn_filters_body(mine_ref, other_ref, w2_ref, wb_ref):
    even = is_even("dev")
    for pair in range(14):
        at = 128 * (pair % 7)
        mine, other = mine_ref[:, at : at + 128].astype(F32), other_ref[:, at : at + 128].astype(F32)
        block = jnp.where(even, mine, other) if pair < 7 else jnp.where(even, other, mine)
        w2_ref[:, 128 * pair : 128 * pair + 128] = block.astype(BF)
        turned = jnp.transpose(block, (1, 0)).astype(BF)
        wb_ref[:, 256 * pair : 256 * pair + 128] = turned[0:64, :]
        if pair < 13:
            wb_ref[:, 256 * pair + 128 : 256 * pair + 256] = turned[64:128, :]


def backward_body(delta_ref, wb_ref, slope_ref, image_ref, low_ref, rim_ref, pooled_ref, keep_ref, give_ref, pd, one):
    for a in range(3):
        for (b, e), value in shifted(delta_ref[128 * a : 128 * a + 128, :].astype(F32)):
            t = 26 - (a * 9 + b * 3 + e)
            pd[128 * t : 128 * t + 128, :] = value.astype(BF)
    back = mm(wb_ref[...], pd[...])
    for r in range(4):
        turned = back if r == 0 else pltpu.roll(back, 256 - 64 * r, 1)
        pooled_ref[:, r, :] = turned[:, 0:64].astype(BF)
    w_in, n_out = rows_of((128, 256)), lanes((128, 256))
    total = jnp.zeros((64, 1024), F32)
    grown = []
    for pair in range(2):
        grow = (w_in == n_out // 2).astype(F32).astype(BF)
        grown.append(split_mm(back[:, 128 * pair : 128 * pair + 128], grow, 3))
    for i in range(2):
        for jp in range(4):
            row = grown[jp // 2][:, 128 * (jp % 2) : 128 * (jp % 2) + 128]
            at = (i * 4 + jp) * 256
            delta = (jnp.concatenate([row, row], axis=1) * slope_ref[:, at : at + 256]).astype(BF)
            cells = patches_one(image_ref, low_ref, rim_ref, i, jp)
            blank = jnp.zeros((32, 256), BF)
            chunks = []
            for s in range(4):
                chunks += [cells[224 * s : min(224 * s + 224, 864), :], blank]
            chunks.append(blank)
            total = total + mm_nt(delta, jnp.concatenate(chunks, axis=0))
    for s in range(4):
        for quarter in range(4):
            for side in range(2):
                at = 256 * s + 128 * side
                one[side, pl.ds(s * 4 + quarter, 16, stride=16), :] = total[16 * quarter : 16 * quarter + 16, at : at + 128]
    even = is_even("dev")
    for c in range(8):
        for side in range(2):
            at = 128 * side
            first, second = one[side, 32 * c : 32 * c + 16, :], one[side, 32 * c + 16 : 32 * c + 32, :]
            keep_ref[16 * c : 16 * c + 16, at : at + 128] = jnp.where(even, first, second)
            give_ref[16 * c : 16 * c + 16, at : at + 128] = jnp.where(even, second, first).astype(BF)


def sum_chip_body(two_ref, other_two_ref, one_ref, other_one_ref, out_ref):
    out_ref[:, 0:896] = (two_ref[...] + other_two_ref[...].astype(F32)).astype(BF)
    out_ref[:, 896:1152] = (one_ref[...] + other_one_ref[...].astype(F32)).astype(BF)


def sum_depth_body(in_ref, act_ref, out_ref, acc):
    total = in_ref[0:16, :].astype(F32)
    for d in range(1, 8):
        total = total + in_ref[16 * d : 16 * d + 16, :].astype(F32)
    act = act_ref[...].astype(F32)
    acc[...] = jnp.zeros(acc.shape, F32)
    for m in range(7):
        acc[1, pl.ds(m, 16, stride=16), :] = total[:, 128 * m : 128 * m + 128]
    for h in range(16):
        for side in range(2):
            at = 16 * h + 8 * side
            acc[0, at : at + 8, :] = act[8 * h : 8 * h + 8, 128 * side : 128 * side + 128]
    out_ref[:, 256:384] = acc[0].astype(BF)
    out_ref[:, 384:512] = acc[1].astype(BF)
    one = total[:, 896:1152].astype(BF)
    for h in range(16):
        out_ref[16 * h : 16 * h + 16, 0:256] = one


def sum_height_body(in_ref, act_ref, out_ref, acc):
    one, two = None, None
    for h in range(16):
        block = in_ref[16 * h : 16 * h + 16, :].astype(F32)
        one = block[:, 0:256] if h == 0 else one + block[:, 0:256]
        two = block[:, 384:512] if h == 0 else two + block[:, 384:512]
        for r in range(4):
            value = block[8 * (r // 2) : 8 * (r // 2) + 8, 256:384]
            acc[pl.ds(4 * h + r, 8, stride=64), :] = pltpu.roll(value, 64, 1) if r % 2 else value
    act_ref[...] = acc[...][:, 0:64].astype(BF)
    packed = jnp.concatenate([one, two], axis=1).astype(BF)
    for d in range(16):
        out_ref[16 * d : 16 * d + 16, :] = packed


def finish_body(in_ref, one_ref, two_ref, acc):
    for part in range(3):
        acc[part, :, :] = in_ref[:, 128 * part : 128 * part + 128].astype(F32)
    for half in range(2):
        for m in range(7):
            value = acc[2, pl.ds(16 * half + m, 8, stride=32), :] * (1.0 / math.sqrt(CELLS_TWO))
            t = 14 * half + 2 * m
            two_ref[t] = value[:, 0:64]
            if t + 1 < 27:
                two_ref[t + 1] = pltpu.roll(value, 64, 1)[:, 0:64]
    scale = 8.0 / math.sqrt(CELLS_ONE)
    for s in range(4):
        for side in range(2):
            rows = [acc[side, pl.ds(s * 4 + quarter, 16, stride=16), :] for quarter in range(4)]
            turned = jnp.transpose(jnp.concatenate(rows, axis=0), (1, 0)) * scale
            for k in range(4):
                t = 7 * s + 4 * side + k
                if 4 * side + k < 7 and t < 27:
                    one_ref[t] = turned[32 * k : 32 * k + 32, :]


def move(block, axis, step):
    size = lax.axis_size(axis)
    return lax.ppermute(block, axis, [(i, i + step) for i in range(size) if 0 <= i + step < size])


def swap(block, axis, first):
    pairs = [(i, i + 1) for i in range(first, lax.axis_size(axis) - 1, 2)]
    return lax.ppermute(block, axis, pairs + [(j, i) for i, j in pairs])


def exchange(block, axis, groups=None):
    return lax.all_to_all(block, axis, 0, 0, tiled=True, axis_index_groups=groups)


def shards(image, kernel_one, kernel_two, cotangent):
    x = image.reshape(2048, 256)
    k1 = jnp.transpose(kernel_one, (2, 3, 4, 1, 0)).reshape(864, 64)
    k2 = jnp.transpose(kernel_two, (2, 3, 4, 0, 1)).reshape(27, 8, 64)
    cot = cotangent.reshape(512, 64)
    plane, row, corner, packed = call(
        pack_body,
        [shape((512, 256), BF), shape((128, 256), BF), shape((32, 256), BF), shape((128, 1280), BF)],
        [x, k2, cot],
        [
            pltpu.VMEM((2048, 256), BF),
            pltpu.VMEM((27, 8, 64), BF),
            pltpu.VMEM((512, 64), BF),
            pltpu.VMEM((2, 1024, 128), F32),
            pltpu.VMEM((128, 1280), F32),
            pltpu.VMEM((512, 128), F32),
            pltpu.SemaphoreType.DMA((3,)),
        ],
        space=pl.ANY,
        limit=60 * 1024 * 1024,
    )
    plane = move(plane, "dev", 1)
    row = move(row, "ha", 1)
    n_dev, n_ha = lax.axis_size("dev"), lax.axis_size("ha")
    corner = lax.ppermute(
        corner,
        ("dev", "ha"),
        [(d * n_ha + h, (d + 1) * n_ha + h + 1) for d in range(n_dev - 1) for h in range(n_ha - 1)],
    )
    a2 = exchange(packed, "ha")
    own, wt = call(
        turn_image_body,
        [shape((64, 96, 128), BF), shape((64, 864), BF)],
        [x, k1],
        [pltpu.VMEM((2048, 128), F32), pltpu.VMEM((2048, 128), F32)],
        flops=300000000,
    )
    slope, pooled, low, top = call(
        first_layer_body,
        [
            shape((64, 2048), F32),
            shape((64, 256), BF),
            shape((16, 96, 128), BF),
            shape((5, 96, 128), BF),
        ],
        [own, wt, plane, row, corner],
        [pltpu.VMEM((672, 128), F32), pltpu.VMEM((672, 128), F32)],
        flops=400000000,
    )
    other = swap(pooled, "dev", 0)
    (rims,) = call(rims_body, [shape((128, 128), BF)], [pooled, other])
    route = []
    for d in range(n_dev):
        for h in range(d % 2, n_ha - 1, 2):
            route += [(d * n_ha + h, d * n_ha + h + 1), (d * n_ha + h + 1, d * n_ha + h)]
    rims = lax.ppermute(rims, ("dev", "ha"), route)
    a2_other = swap(a2, "dev", 0)
    w2, wb = call(turn_filters_body, [shape((128, 1792), BF), shape((64, 3456), BF)], [a2, a2_other])
    (pair,) = call(widen_body, [shape((128, 896), BF)], [pooled, other, rims, swap(rims, "dev", 0), a2])
    cross = swap(pair, "dev", 1)
    patches, act, delta = call(
        second_layer_body,
        [shape((2944, 384), BF), shape((128, 256), BF), shape((384, 384), BF)],
        [pair, cross, swap(cross, "dev", 0), w2, a2_other],
        flops=500000000,
    )
    keep_two, give_two = call(
        grad_two_body, [shape((128, 896), F32), shape((128, 896), BF)], [delta, patches], flops=180000000
    )
    grad_pooled, keep_one, give_one = call(
        backward_body,
        [shape((64, 4, 64), BF), shape((128, 256), F32), shape((128, 256), BF)],
        [delta, wb, slope, own, low, top],
        [pltpu.VMEM((3456, 256), BF), pltpu.VMEM((2, 256, 128), F32)],
        flops=400000000,
    )
    (first,) = call(
        sum_chip_body,
        [shape((128, 1152), BF)],
        [keep_two, swap(give_two, "dev", 0), keep_one, swap(give_one, "dev", 0)],
    )
    same_core = [list(range(core, lax.axis_size("dev"), 2)) for core in range(2)]
    (second,) = call(
        sum_depth_body,
        [shape((256, 512), BF)],
        [exchange(first, "dev", same_core), act],
        [pltpu.VMEM((2, 256, 128), F32)],
    )
    activation, third = call(
        sum_height_body,
        [shape((512, 64), BF), shape((256, 384), BF)],
        [exchange(second, "ha")],
        [pltpu.VMEM((512, 128), F32)],
    )
    one, two = call(
        finish_body,
        [shape((27, 32, 64), F32), shape((27, 8, 64), F32)],
        [exchange(third, "dev")],
        [pltpu.VMEM((3, 256, 128), F32)],
    )
    grad_one = jnp.transpose(one.reshape(3, 3, 3, 32, 64), (4, 3, 0, 1, 2))
    grad_two = jnp.transpose(two.reshape(3, 3, 3, 8, 64), (3, 4, 0, 1, 2))
    return (activation.reshape(8, 1, 64, 64), grad_pooled.reshape(64, 1, 4, 64), grad_one, grad_two)


def solution(mesh):
    return jax.shard_map(
        shards,
        mesh=mesh,
        in_specs=(
            P(None, "dev", "ha", None),
            P(),
            P("ha", None, None, None, None),
            P("ha", "dev", None, None),
        ),
        out_specs=(
            P("ha", "dev", None, None),
            P(None, "dev", "ha", None),
            P(),
            P("ha", None, None, None, None),
        ),
        check_vma=False,
    )
```

```python
import math

import jax
import jax.numpy as jnp
from jax import lax
from jax.experimental import pallas as pl
from jax.experimental.pallas import tpu as pltpu
from jax.sharding import PartitionSpec as P

BF = jnp.bfloat16
F32 = jnp.float32
CELLS_ONE = 524288
CELLS_TWO = 65536
VMEM_LIMIT = 32 * 1024 * 1024


def call(body, out_shape, args, scratch=(), flops=1000000, space=pltpu.VMEM, limit=VMEM_LIMIT):
    moved = sum(math.prod(s.shape) * s.dtype.itemsize for s in list(out_shape) + list(args))
    return pl.pallas_call(
        body,
        out_shape=out_shape,
        in_specs=[pl.BlockSpec(memory_space=space)] * len(args),
        out_specs=[pl.BlockSpec(memory_space=pltpu.VMEM)] * len(out_shape),
        scratch_shapes=scratch,
        compiler_params=pltpu.CompilerParams(vmem_limit_bytes=limit),
        cost_estimate=pl.CostEstimate(flops=flops, bytes_accessed=moved, transcendentals=0),
    )(*args)


def shape(dims, dtype):
    return jax.ShapeDtypeStruct(dims, dtype)


def lanes(dims):
    return lax.broadcasted_iota(jnp.int32, dims, len(dims) - 1)


def rows_of(dims):
    return lax.broadcasted_iota(jnp.int32, dims, len(dims) - 2)


def mm(a, b):
    return lax.dot_general(a, b, (((1,), (0,)), ((), ())), preferred_element_type=F32)


def mm_nt(a, b):
    return lax.dot_general(a, b, (((1,), (1,)), ((), ())), preferred_element_type=F32)


def split_mm(a, sel, terms):
    total = None
    for _ in range(terms):
        part = a.astype(BF)
        a = a - part.astype(F32)
        term = mm(part, sel)
        total = term if total is None else total + term
    return total


def pack_body(x_hbm, k_hbm, cot_hbm, plane_ref, row_ref, corner_ref, out_ref, x_ref, k_ref, cot_ref, last, acc, cots, sems):
    copies = []
    for i, (src, dst) in enumerate([(x_hbm, x_ref), (k_hbm, k_ref), (cot_hbm, cot_ref)]):
        copies.append(pltpu.make_async_copy(src, dst, sems.at[i]))
        copies[i].start()
    copies[1].wait()
    even = is_even("dev")
    pieces = []
    for pair in range(7):
        taps = []
        for t in (2 * pair, 2 * pair + 1):
            high = k_ref[t + 14].astype(F32) if t < 13 else jnp.zeros((8, 64), F32)
            taps.append(jnp.where(even, k_ref[t].astype(F32), high))
        pieces.append(jnp.concatenate(taps, axis=1))
    filters = jnp.concatenate(pieces, axis=1)
    for h in range(16):
        acc[8 * h : 8 * h + 8, 0:896] = filters
    copies[2].wait()
    cots[...] = jnp.concatenate([cot_ref[...].astype(F32), jnp.zeros((512, 64), F32)], axis=1)
    for h in range(16):
        for part in range(3):
            two = []
            for row in (4 * h - 1 + 2 * part, 4 * h + 2 * part):
                two.append(cots[pl.ds(row, 8, stride=64), :] if 0 <= row < 64 else jnp.zeros((8, 128), F32))
            at = 896 + 128 * part
            acc[8 * h : 8 * h + 8, at : at + 128] = two[0] + pltpu.roll(two[1], 64, 1)
    out_ref[...] = acc[...].astype(BF)
    copies[0].wait()
    for c in range(32):
        plane_ref[16 * c : 16 * c + 16, :] = x_ref[64 * c + 48 : 64 * c + 64, :]
    for part in range(128):
        block = x_ref[16 * part : 16 * part + 16, :].astype(F32)[8:16]
        for side in range(2):
            last[side, 8 * part : 8 * part + 8, :] = block[:, 128 * side : 128 * side + 128]
    for side in range(2):
        at = 128 * side
        row_ref[:, at : at + 128] = last[side, pl.ds(7, 128, stride=8), :].astype(BF)
        corner_ref[:, at : at + 128] = last[side, pl.ds(31, 32, stride=32), :].astype(BF)


def parted(value, ev, od, at):
    w_in, n_out = rows_of((256, 256)), lanes((256, 256))
    sel = (w_in == jnp.where(n_out < 128, 2 * n_out, 2 * n_out - 255)).astype(F32).astype(BF)
    both = mm(value, sel)
    ev[at : at + value.shape[0], :] = both[:, :128]
    od[at : at + value.shape[0], :] = both[:, 128:]


def place(out_ref, index, ev, od, start, stride):
    even = ev[pl.ds(start, 32, stride=stride), :]
    odd = od[pl.ds(start, 32, stride=stride), :]
    before = jnp.where(lanes((32, 128)) == 0, 0.0, pltpu.roll(odd, 1, 1))
    out_ref[index, 0:32, :] = before.astype(BF)
    out_ref[index, 32:64, :] = even.astype(BF)
    out_ref[index, 64:96, :] = odd.astype(BF)


def turn_image_body(x_ref, w_ref, own_ref, wt_ref, ev, od):
    for part in range(8):
        parted(x_ref[256 * part : 256 * part + 256, :], ev, od, 256 * part)
    for row in range(64):
        place(own_ref, row, ev, od, row, 64)
    wt_ref[...] = jnp.transpose(w_ref[...].astype(F32), (1, 0)).astype(BF)


def first_layer_body(own_ref, wt_ref, plane_ref, row_ref, corner_ref, slope_ref, pooled_ref, low_ref, top_ref, ev, od):
    for part in range(2):
        parted(plane_ref[256 * part : 256 * part + 256, :], ev, od, 256 * part)
    parted(row_ref[...], ev, od, 512)
    parted(corner_ref[...], ev, od, 640)
    for r in range(16):
        place(low_ref, r, ev, od, r, 16)
    place(top_ref, 0, ev, od, 640, 1)
    for p in range(4):
        place(top_ref, 1 + p, ev, od, 512 + p, 4)
    weights = wt_ref[...]
    sums = [None] * 4
    for i in range(2):
        for jp in range(4):
            pre = mm(weights, patches_one(own_ref, low_ref, top_ref, i, jp))
            sigma = jax.nn.sigmoid(pre)
            at = (i * 4 + jp) * 256
            slope_ref[:, at : at + 256] = sigma * (1.0 + pre * (1.0 - sigma)) * 0.125
            act = pre * sigma
            both = act[:, :128] + act[:, 128:]
            sums[jp] = both if i == 0 else sums[jp] + both
    k_in, k_out = rows_of((256, 128)), lanes((256, 128))
    fold = ((k_in // 2) == k_out).astype(F32).astype(BF)
    halves = []
    for pair in range(2):
        stacked = jnp.concatenate([sums[2 * pair], sums[2 * pair + 1]], axis=1)
        halves.append(split_mm(stacked, fold, 3) * 0.125)
    pooled = jnp.concatenate(halves, axis=1)
    pooled_ref[...] = pooled.astype(BF)


def patches_one(own_ref, low_ref, top_ref, i, jp):
    def block(a, b):
        if b == 0:
            return top_ref[a]
        return low_ref[b - 1] if a == 0 else own_ref[(a - 1) * 16 + b - 1]

    columns = []
    for j in (2 * jp, 2 * jp + 1):
        columns.append(jnp.concatenate([block(2 * i + a, 2 * j + b) for a in range(3) for b in range(3)], axis=0))
    return jnp.concatenate(columns, axis=1)


def is_even(axis):
    return lax.axis_index(axis) % 2 == 0


def shifted(ext):
    width = ext.shape[1]
    kept = width - 128
    column = lanes(ext.shape) & 63
    for e in range(3):
        if e == 0:
            moved = jnp.where(column == 0, 0.0, pltpu.roll(ext, 1, 1))
        elif e == 2:
            moved = jnp.where(column == 63, 0.0, pltpu.roll(ext, width - 1, 1))
        else:
            moved = ext
        yield (0, e), moved[:, 0:kept]
        yield (1, e), pltpu.roll(moved, width - 64, 1)[:, 0:kept]
        yield (2, e), moved[:, 128:width]


def rims_body(own_ref, other_ref, out_ref):
    bottom = is_even("ha") == is_even("dev")
    for k, ref in enumerate((own_ref, other_ref)):
        value = ref[...].astype(F32)
        out_ref[64 * k : 64 * k + 64, :] = jnp.where(bottom, value[:, 128:256], value[:, 0:128]).astype(BF)


def widen_body(own_ref, other_ref, mine_ref, core_ref, out_ref):
    swapped = is_even("ha") == is_even("dev")
    mine, core = mine_ref[...].astype(F32), core_ref[...].astype(F32)
    for k, ref in enumerate((own_ref, other_ref)):
        here, there = mine[64 * k : 64 * k + 64], core[64 - 64 * k : 128 - 64 * k]
        out_ref[64 * k : 64 * k + 64, 0:128] = jnp.where(swapped, there, here).astype(BF)
        out_ref[64 * k : 64 * k + 64, 128:384] = ref[...]
        out_ref[64 * k : 64 * k + 64, 384:512] = jnp.where(swapped, here, there).astype(BF)


def second_layer_body(pair_ref, cross_ref, core_ref, w2_ref, a2_ref, other_ref, cot_ref, patches_ref, act_ref, delta_ref):
    even = is_even("dev")

    def planes(ref):
        return ref[0:64, 0:512].astype(F32), ref[64:128, 0:512].astype(F32)

    own, other = planes(pair_ref)
    near, far = planes(cross_ref)
    beyond = core_ref[0:64, 0:512].astype(F32)
    ordered = (
        jnp.where(even, far, beyond),
        jnp.where(even, near, other),
        own,
        jnp.where(even, other, near),
        jnp.where(even, beyond, far),
    )
    for a, plane in enumerate(ordered):
        for (b, e), value in shifted(plane):
            t = a * 9 + b * 3 + e
            patches_ref[64 * t : 64 * t + 64, :] = value.astype(BF)
    patches_ref[2880:2944, :] = jnp.zeros((64, 384), BF)
    cot_cross, cot_core = cot_ref[...].astype(F32), other_ref[:, 896:1280].astype(F32)
    cots = (
        jnp.where(even, cot_cross, cot_core),
        a2_ref[:, 896:1280].astype(F32),
        jnp.where(even, cot_core, cot_cross),
    )
    for p in range(3):
        pre = mm(w2_ref[...], patches_ref[576 * p : 576 * p + 1792, :])
        sigma = jax.nn.sigmoid(pre)
        if p == 1:
            act_ref[...] = pltpu.roll(pre * sigma, 320, 1)[:, 0:256].astype(BF)
        slope = sigma * (1.0 + pre * (1.0 - sigma))
        delta_ref[128 * p : 128 * p + 128, :] = (cots[p] * slope).astype(BF)


def grad_two_body(delta_ref, patches_ref, keep_ref, give_ref):
    r, o = rows_of((128, 128)), lanes((128, 128))
    order = (o == (r % 16) * 8 + r // 16).astype(F32).astype(BF)
    cell = lanes((128, 384))
    mine = (cell >= 64) & (cell < 320)
    delta = jnp.where(mine, mm(order, delta_ref[128:256, :]), 0.0).astype(BF)
    grad = mm_nt(delta, patches_ref[576:2368, :])
    even = is_even("dev")
    keep_ref[...] = jnp.where(even, grad[:, 0:896], grad[:, 896:1792])
    give_ref[...] = jnp.where(even, grad[:, 896:1792], grad[:, 0:896]).astype(BF)


def turn_filters_body(mine_ref, other_ref, w2_ref, wb_ref):
    even = is_even("dev")
    for pair in range(14):
        at = 128 * (pair % 7)
        mine, other = mine_ref[:, at : at + 128].astype(F32), other_ref[:, at : at + 128].astype(F32)
        block = jnp.where(even, mine, other) if pair < 7 else jnp.where(even, other, mine)
        w2_ref[:, 128 * pair : 128 * pair + 128] = block.astype(BF)
        turned = jnp.transpose(block, (1, 0)).astype(BF)
        wb_ref[:, 256 * pair : 256 * pair + 128] = turned[0:64, :]
        if pair < 13:
            wb_ref[:, 256 * pair + 128 : 256 * pair + 256] = turned[64:128, :]


def backward_body(delta_ref, wb_ref, slope_ref, image_ref, low_ref, rim_ref, pooled_ref, keep_ref, give_ref, pd, one):
    for a in range(3):
        for (b, e), value in shifted(delta_ref[128 * a : 128 * a + 128, :].astype(F32)):
            t = 26 - (a * 9 + b * 3 + e)
            pd[128 * t : 128 * t + 128, :] = value.astype(BF)
    back = mm(wb_ref[...], pd[...])
    for r in range(4):
        turned = back if r == 0 else pltpu.roll(back, 256 - 64 * r, 1)
        pooled_ref[:, r, :] = turned[:, 0:64].astype(BF)
    w_in, n_out = rows_of((128, 256)), lanes((128, 256))
    total = jnp.zeros((64, 1024), F32)
    grown = []
    for pair in range(2):
        grow = (w_in == n_out // 2).astype(F32).astype(BF)
        grown.append(split_mm(back[:, 128 * pair : 128 * pair + 128], grow, 3))
    for i in range(2):
        for jp in range(4):
            row = grown[jp // 2][:, 128 * (jp % 2) : 128 * (jp % 2) + 128]
            at = (i * 4 + jp) * 256
            delta = (jnp.concatenate([row, row], axis=1) * slope_ref[:, at : at + 256]).astype(BF)
            cells = patches_one(image_ref, low_ref, rim_ref, i, jp)
            blank = jnp.zeros((32, 256), BF)
            chunks = []
            for s in range(4):
                chunks += [cells[224 * s : min(224 * s + 224, 864), :], blank]
            chunks.append(blank)
            total = total + mm_nt(delta, jnp.concatenate(chunks, axis=0))
    for s in range(4):
        for quarter in range(4):
            for side in range(2):
                at = 256 * s + 128 * side
                one[side, pl.ds(s * 4 + quarter, 16, stride=16), :] = total[16 * quarter : 16 * quarter + 16, at : at + 128]
    even = is_even("dev")
    for c in range(8):
        for side in range(2):
            at = 128 * side
            first, second = one[side, 32 * c : 32 * c + 16, :], one[side, 32 * c + 16 : 32 * c + 32, :]
            keep_ref[16 * c : 16 * c + 16, at : at + 128] = jnp.where(even, first, second)
            give_ref[16 * c : 16 * c + 16, at : at + 128] = jnp.where(even, second, first).astype(BF)


def sum_chip_body(two_ref, other_two_ref, one_ref, other_one_ref, out_ref):
    out_ref[:, 0:896] = (two_ref[...] + other_two_ref[...].astype(F32)).astype(BF)
    out_ref[:, 896:1152] = (one_ref[...] + other_one_ref[...].astype(F32)).astype(BF)


def sum_depth_body(in_ref, act_ref, out_ref, acc):
    total = in_ref[0:16, :].astype(F32)
    for d in range(1, 8):
        total = total + in_ref[16 * d : 16 * d + 16, :].astype(F32)
    act = act_ref[...].astype(F32)
    acc[...] = jnp.zeros(acc.shape, F32)
    for m in range(7):
        acc[1, pl.ds(m, 16, stride=16), :] = total[:, 128 * m : 128 * m + 128]
    for h in range(16):
        for side in range(2):
            at = 16 * h + 8 * side
            acc[0, at : at + 8, :] = act[8 * h : 8 * h + 8, 128 * side : 128 * side + 128]
    out_ref[:, 256:384] = acc[0].astype(BF)
    out_ref[:, 384:512] = acc[1].astype(BF)
    one = total[:, 896:1152].astype(BF)
    for h in range(16):
        out_ref[16 * h : 16 * h + 16, 0:256] = one


def sum_height_body(in_ref, out_ref):
    one, two = None, None
    for h in range(16):
        block = in_ref[16 * h : 16 * h + 16, :].astype(F32)
        one = block[:, 0:256] if h == 0 else one + block[:, 0:256]
        two = block[:, 384:512] if h == 0 else two + block[:, 384:512]
    packed = jnp.concatenate([one, two], axis=1).astype(BF)
    for c in range(8):
        out_ref[16 * c : 16 * c + 16, :] = packed


def lay_activation_body(in_ref, act_ref, acc):
    for h in range(16):
        block = in_ref[16 * h : 16 * h + 16, 256:384].astype(F32)
        for r in range(4):
            value = block[8 * (r // 2) : 8 * (r // 2) + 8, :]
            acc[pl.ds(4 * h + r, 8, stride=64), :] = pltpu.roll(value, 64, 1) if r % 2 else value
    act_ref[...] = acc[...][:, 0:64].astype(BF)


def finish_body(mine_ref, other_ref, one_ref, two_ref, acc):
    even = is_even("dev")
    for c in range(8):
        mine = mine_ref[16 * c : 16 * c + 16, :].astype(F32)
        other = other_ref[16 * c : 16 * c + 16, :].astype(F32)
        first, second = jnp.where(even, mine, other), jnp.where(even, other, mine)
        for part in range(3):
            acc[part, 32 * c : 32 * c + 16, :] = first[:, 128 * part : 128 * part + 128]
            acc[part, 32 * c + 16 : 32 * c + 32, :] = second[:, 128 * part : 128 * part + 128]
    for half in range(2):
        for m in range(7):
            value = acc[2, pl.ds(16 * half + m, 8, stride=32), :] * (1.0 / math.sqrt(CELLS_TWO))
            t = 14 * half + 2 * m
            two_ref[t] = value[:, 0:64]
            if t + 1 < 27:
                two_ref[t + 1] = pltpu.roll(value, 64, 1)[:, 0:64]
    scale = 8.0 / math.sqrt(CELLS_ONE)
    for s in range(4):
        for side in range(2):
            rows = [acc[side, pl.ds(s * 4 + quarter, 16, stride=16), :] for quarter in range(4)]
            turned = jnp.transpose(jnp.concatenate(rows, axis=0), (1, 0)) * scale
            for k in range(4):
                t = 7 * s + 4 * side + k
                if 4 * side + k < 7 and t < 27:
                    one_ref[t] = turned[32 * k : 32 * k + 32, :]


def move(block, axis, step):
    size = lax.axis_size(axis)
    return lax.ppermute(block, axis, [(i, i + step) for i in range(size) if 0 <= i + step < size])


def swap(block, axis, first):
    pairs = [(i, i + 1) for i in range(first, lax.axis_size(axis) - 1, 2)]
    return lax.ppermute(block, axis, pairs + [(j, i) for i, j in pairs])


def exchange(block, axis, groups=None):
    return lax.all_to_all(block, axis, 0, 0, tiled=True, axis_index_groups=groups)


def shards(image, kernel_one, kernel_two, cotangent):
    x = image.reshape(2048, 256)
    k1 = jnp.transpose(kernel_one, (2, 3, 4, 1, 0)).reshape(864, 64)
    k2 = jnp.transpose(kernel_two, (2, 3, 4, 0, 1)).reshape(27, 8, 64)
    cot = cotangent.reshape(512, 64)
    plane, row, corner, packed = call(
        pack_body,
        [shape((512, 256), BF), shape((128, 256), BF), shape((32, 256), BF), shape((128, 1280), BF)],
        [x, k2, cot],
        [
            pltpu.VMEM((2048, 256), BF),
            pltpu.VMEM((27, 8, 64), BF),
            pltpu.VMEM((512, 64), BF),
            pltpu.VMEM((2, 1024, 128), F32),
            pltpu.VMEM((128, 1280), F32),
            pltpu.VMEM((512, 128), F32),
            pltpu.SemaphoreType.DMA((3,)),
        ],
        space=pl.ANY,
        limit=60 * 1024 * 1024,
    )
    plane = move(plane, "dev", 1)
    row = move(row, "ha", 1)
    n_dev, n_ha = lax.axis_size("dev"), lax.axis_size("ha")
    corner = lax.ppermute(
        corner,
        ("dev", "ha"),
        [(d * n_ha + h, (d + 1) * n_ha + h + 1) for d in range(n_dev - 1) for h in range(n_ha - 1)],
    )
    a2 = exchange(packed, "ha")
    own, wt = call(
        turn_image_body,
        [shape((64, 96, 128), BF), shape((64, 864), BF)],
        [x, k1],
        [pltpu.VMEM((2048, 128), F32), pltpu.VMEM((2048, 128), F32)],
        flops=300000000,
    )
    slope, pooled, low, top = call(
        first_layer_body,
        [
            shape((64, 2048), F32),
            shape((64, 256), BF),
            shape((16, 96, 128), BF),
            shape((5, 96, 128), BF),
        ],
        [own, wt, plane, row, corner],
        [pltpu.VMEM((672, 128), F32), pltpu.VMEM((672, 128), F32)],
        flops=400000000,
    )
    other = swap(pooled, "dev", 0)
    (rims,) = call(rims_body, [shape((128, 128), BF)], [pooled, other])
    route = []
    for d in range(n_dev):
        for h in range(d % 2, n_ha - 1, 2):
            route += [(d * n_ha + h, d * n_ha + h + 1), (d * n_ha + h + 1, d * n_ha + h)]
    rims = lax.ppermute(rims, ("dev", "ha"), route)
    a2_other = swap(a2, "dev", 0)
    w2, wb = call(turn_filters_body, [shape((128, 1792), BF), shape((64, 3456), BF)], [a2, a2_other])
    cot_cross = swap(a2[:, 896:1280], "dev", 1)
    rims_core, cot_cross = lax.optimization_barrier((swap(rims, "dev", 0), cot_cross))
    (pair,) = call(widen_body, [shape((128, 512), BF)], [pooled, other, rims, rims_core])
    cross = swap(pair, "dev", 1)
    patches, act, delta = call(
        second_layer_body,
        [shape((2944, 384), BF), shape((128, 256), BF), shape((384, 384), BF)],
        [pair, cross, swap(cross, "dev", 0), w2, a2, a2_other, cot_cross],
        flops=500000000,
    )
    keep_two, give_two = call(
        grad_two_body, [shape((128, 896), F32), shape((128, 896), BF)], [delta, patches], flops=180000000
    )
    grad_pooled, keep_one, give_one = call(
        backward_body,
        [shape((64, 4, 64), BF), shape((128, 256), F32), shape((128, 256), BF)],
        [delta, wb, slope, own, low, top],
        [pltpu.VMEM((3456, 256), BF), pltpu.VMEM((2, 256, 128), F32)],
        flops=400000000,
    )
    (first,) = call(
        sum_chip_body,
        [shape((128, 1152), BF)],
        [keep_two, swap(give_two, "dev", 0), keep_one, swap(give_one, "dev", 0)],
    )
    same_core = [list(range(core, lax.axis_size("dev"), 2)) for core in range(2)]
    (second,) = call(
        sum_depth_body,
        [shape((256, 512), BF)],
        [exchange(first, "dev", same_core), act],
        [pltpu.VMEM((2, 256, 128), F32)],
    )
    second = exchange(second, "ha")
    (third,) = call(sum_height_body, [shape((128, 384), BF)], [second])
    (activation,) = call(lay_activation_body, [shape((512, 64), BF)], [second], [pltpu.VMEM((512, 128), F32)])
    third = exchange(third, "dev", same_core)
    one, two = call(
        finish_body,
        [shape((27, 32, 64), F32), shape((27, 8, 64), F32)],
        [third, swap(third, "dev", 0)],
        [pltpu.VMEM((3, 256, 128), F32)],
    )
    grad_one = jnp.transpose(one.reshape(3, 3, 3, 32, 64), (4, 3, 0, 1, 2))
    grad_two = jnp.transpose(two.reshape(3, 3, 3, 8, 64), (3, 4, 0, 1, 2))
    return (activation.reshape(8, 1, 64, 64), grad_pooled.reshape(64, 1, 4, 64), grad_one, grad_two)


def solution(mesh):
    return jax.shard_map(
        shards,
        mesh=mesh,
        in_specs=(
            P(None, "dev", "ha", None),
            P(),
            P("ha", None, None, None, None),
            P("ha", "dev", None, None),
        ),
        out_specs=(
            P("ha", "dev", None, None),
            P(None, "dev", "ha", None),
            P(),
            P("ha", None, None, None, None),
        ),
        check_vma=False,
    )
```

```python
import math

import jax
import jax.numpy as jnp
from jax import lax
from jax.experimental import pallas as pl
from jax.experimental.pallas import tpu as pltpu
from jax.sharding import PartitionSpec as P

BF = jnp.bfloat16
F32 = jnp.float32
CELLS_ONE = 524288
CELLS_TWO = 65536
VMEM_LIMIT = 32 * 1024 * 1024


def call(body, out_shape, args, scratch=(), flops=1000000, space=pltpu.VMEM, limit=VMEM_LIMIT):
    moved = sum(math.prod(s.shape) * s.dtype.itemsize for s in list(out_shape) + list(args))
    return pl.pallas_call(
        body,
        out_shape=out_shape,
        in_specs=[pl.BlockSpec(memory_space=space)] * len(args),
        out_specs=[pl.BlockSpec(memory_space=pltpu.VMEM)] * len(out_shape),
        scratch_shapes=scratch,
        compiler_params=pltpu.CompilerParams(vmem_limit_bytes=limit),
        cost_estimate=pl.CostEstimate(flops=flops, bytes_accessed=moved, transcendentals=0),
    )(*args)


def shape(dims, dtype):
    return jax.ShapeDtypeStruct(dims, dtype)


def lanes(dims):
    return lax.broadcasted_iota(jnp.int32, dims, len(dims) - 1)


def rows_of(dims):
    return lax.broadcasted_iota(jnp.int32, dims, len(dims) - 2)


def mm(a, b):
    return lax.dot_general(a, b, (((1,), (0,)), ((), ())), preferred_element_type=F32)


def mm_nt(a, b):
    return lax.dot_general(a, b, (((1,), (1,)), ((), ())), preferred_element_type=F32)


def split_mm(a, sel, terms):
    total = None
    for _ in range(terms):
        part = a.astype(BF)
        a = a - part.astype(F32)
        term = mm(part, sel)
        total = term if total is None else total + term
    return total


def pack_body(x_hbm, k_hbm, cot_hbm, plane_ref, row_ref, corner_ref, out_ref, x_ref, k_ref, cot_ref, last, acc, cots, sems):
    copies = []
    for i, (src, dst) in enumerate([(x_hbm, x_ref), (k_hbm, k_ref), (cot_hbm, cot_ref)]):
        copies.append(pltpu.make_async_copy(src, dst, sems.at[i]))
        copies[i].start()
    copies[1].wait()
    even = is_even("dev")
    pieces = []
    for pair in range(7):
        taps = []
        for t in (2 * pair, 2 * pair + 1):
            high = k_ref[t + 14].astype(F32) if t < 13 else jnp.zeros((8, 64), F32)
            taps.append(jnp.where(even, k_ref[t].astype(F32), high))
        pieces.append(jnp.concatenate(taps, axis=1))
    filters = jnp.concatenate(pieces, axis=1)
    for h in range(16):
        acc[8 * h : 8 * h + 8, 0:896] = filters
    copies[2].wait()
    cots[0:512, :] = jnp.concatenate([cot_ref[...].astype(F32), jnp.zeros((512, 64), F32)], axis=1)
    for h in range(16):
        for part in range(3):
            two = []
            for row in (4 * h - 1 + 2 * part, 4 * h + 2 * part):
                two.append(cots[pl.ds(row, 8, stride=64), :] if 0 <= row < 64 else jnp.zeros((8, 128), F32))
            at = 896 + 128 * part
            acc[8 * h : 8 * h + 8, at : at + 128] = two[0] + pltpu.roll(two[1], 64, 1)
    out_ref[...] = acc[...].astype(BF)
    copies[0].wait()
    for c in range(32):
        plane_ref[16 * c : 16 * c + 16, :] = x_ref[64 * c + 48 : 64 * c + 64, :]
    for part in range(128):
        block = x_ref[16 * part : 16 * part + 16, :].astype(F32)[8:16]
        for side in range(2):
            last[side, 8 * part : 8 * part + 8, :] = block[:, 128 * side : 128 * side + 128]
    for side in range(2):
        at = 128 * side
        row_ref[:, at : at + 128] = last[side, pl.ds(7, 128, stride=8), :].astype(BF)
        corner_ref[:, at : at + 128] = last[side, pl.ds(31, 32, stride=32), :].astype(BF)


def parted(value, ev, od, at):
    w_in, n_out = rows_of((256, 256)), lanes((256, 256))
    sel = (w_in == jnp.where(n_out < 128, 2 * n_out, 2 * n_out - 255)).astype(F32).astype(BF)
    both = mm(value, sel)
    ev[at : at + value.shape[0], :] = both[:, :128]
    od[at : at + value.shape[0], :] = both[:, 128:]


def place(out_ref, index, ev, od, start, stride):
    even = ev[pl.ds(start, 32, stride=stride), :]
    odd = od[pl.ds(start, 32, stride=stride), :]
    before = jnp.where(lanes((32, 128)) == 0, 0.0, pltpu.roll(odd, 1, 1))
    out_ref[index, 0:32, :] = before.astype(BF)
    out_ref[index, 32:64, :] = even.astype(BF)
    out_ref[index, 64:96, :] = odd.astype(BF)


def turn_image_body(x_ref, w_ref, own_ref, wt_ref, ev, od):
    for part in range(8):
        parted(x_ref[256 * part : 256 * part + 256, :], ev, od, 256 * part)
    for row in range(64):
        place(own_ref, row, ev, od, row, 64)
    wt_ref[...] = jnp.transpose(w_ref[...].astype(F32), (1, 0)).astype(BF)


def first_layer_body(own_ref, wt_ref, plane_ref, row_ref, corner_ref, slope_ref, pooled_ref, low_ref, top_ref, ev, od):
    for part in range(2):
        parted(plane_ref[256 * part : 256 * part + 256, :], ev, od, 256 * part)
    parted(row_ref[...], ev, od, 512)
    parted(corner_ref[...], ev, od, 640)
    for r in range(16):
        place(low_ref, r, ev, od, r, 16)
    place(top_ref, 0, ev, od, 640, 1)
    for p in range(4):
        place(top_ref, 1 + p, ev, od, 512 + p, 4)
    weights = wt_ref[...]
    sums = [None] * 4
    for i in range(2):
        for jp in range(4):
            pre = mm(weights, patches_one(own_ref, low_ref, top_ref, i, jp))
            sigma = jax.nn.sigmoid(pre)
            at = (i * 4 + jp) * 256
            slope_ref[:, at : at + 256] = sigma * (1.0 + pre * (1.0 - sigma)) * 0.125
            act = pre * sigma
            both = act[:, :128] + act[:, 128:]
            sums[jp] = both if i == 0 else sums[jp] + both
    k_in, k_out = rows_of((256, 128)), lanes((256, 128))
    fold = ((k_in // 2) == k_out).astype(F32).astype(BF)
    halves = []
    for pair in range(2):
        stacked = jnp.concatenate([sums[2 * pair], sums[2 * pair + 1]], axis=1)
        halves.append(split_mm(stacked, fold, 3) * 0.125)
    pooled = jnp.concatenate(halves, axis=1)
    pooled_ref[...] = pooled.astype(BF)


def patches_one(own_ref, low_ref, top_ref, i, jp):
    def block(a, b):
        if b == 0:
            return top_ref[a]
        return low_ref[b - 1] if a == 0 else own_ref[(a - 1) * 16 + b - 1]

    columns = []
    for j in (2 * jp, 2 * jp + 1):
        columns.append(jnp.concatenate([block(2 * i + a, 2 * j + b) for a in range(3) for b in range(3)], axis=0))
    return jnp.concatenate(columns, axis=1)


def is_even(axis):
    return lax.axis_index(axis) % 2 == 0


def shifted(ext):
    width = ext.shape[1]
    kept = width - 128
    column = lanes(ext.shape) & 63
    for e in range(3):
        if e == 0:
            moved = jnp.where(column == 0, 0.0, pltpu.roll(ext, 1, 1))
        elif e == 2:
            moved = jnp.where(column == 63, 0.0, pltpu.roll(ext, width - 1, 1))
        else:
            moved = ext
        yield (0, e), moved[:, 0:kept]
        yield (1, e), pltpu.roll(moved, width - 64, 1)[:, 0:kept]
        yield (2, e), moved[:, 128:width]


def rims_body(own_ref, other_ref, out_ref):
    bottom = is_even("ha") == is_even("dev")
    for k, ref in enumerate((own_ref, other_ref)):
        value = ref[...].astype(F32)
        out_ref[64 * k : 64 * k + 64, :] = jnp.where(bottom, value[:, 128:256], value[:, 0:128]).astype(BF)


def widen_body(own_ref, other_ref, mine_ref, core_ref, out_ref):
    swapped = is_even("ha") == is_even("dev")
    mine, core = mine_ref[...].astype(F32), core_ref[...].astype(F32)
    for k, ref in enumerate((own_ref, other_ref)):
        here, there = mine[64 * k : 64 * k + 64], core[64 - 64 * k : 128 - 64 * k]
        out_ref[64 * k : 64 * k + 64, 0:128] = jnp.where(swapped, there, here).astype(BF)
        out_ref[64 * k : 64 * k + 64, 128:384] = ref[...]
        out_ref[64 * k : 64 * k + 64, 384:512] = jnp.where(swapped, here, there).astype(BF)


def second_layer_body(pair_ref, cross_ref, core_ref, w2_ref, a2_ref, other_ref, cot_ref, patches_ref, act_ref, delta_ref):
    even = is_even("dev")

    def planes(ref):
        return ref[0:64, 0:512].astype(F32), ref[64:128, 0:512].astype(F32)

    own, other = planes(pair_ref)
    near, far = planes(cross_ref)
    beyond = core_ref[0:64, 0:512].astype(F32)
    ordered = (
        jnp.where(even, far, beyond),
        jnp.where(even, near, other),
        own,
        jnp.where(even, other, near),
        jnp.where(even, beyond, far),
    )
    for a, plane in enumerate(ordered):
        for (b, e), value in shifted(plane):
            t = a * 9 + b * 3 + e
            patches_ref[64 * t : 64 * t + 64, :] = value.astype(BF)
    patches_ref[2880:2944, :] = jnp.zeros((64, 384), BF)
    cot_cross, cot_core = cot_ref[...].astype(F32), other_ref[:, 896:1280].astype(F32)
    cots = (
        jnp.where(even, cot_cross, cot_core),
        a2_ref[:, 896:1280].astype(F32),
        jnp.where(even, cot_core, cot_cross),
    )
    for p in range(3):
        pre = mm(w2_ref[...], patches_ref[576 * p : 576 * p + 1792, :])
        sigma = jax.nn.sigmoid(pre)
        if p == 1:
            act_ref[...] = pltpu.roll(pre * sigma, 320, 1)[:, 0:256].astype(BF)
        slope = sigma * (1.0 + pre * (1.0 - sigma))
        delta_ref[128 * p : 128 * p + 128, :] = (cots[p] * slope).astype(BF)


def grad_two_body(delta_ref, patches_ref, keep_ref, give_ref):
    r, o = rows_of((128, 128)), lanes((128, 128))
    order = (o == (r % 16) * 8 + r // 16).astype(F32).astype(BF)
    cell = lanes((128, 384))
    mine = (cell >= 64) & (cell < 320)
    delta = jnp.where(mine, mm(order, delta_ref[128:256, :]), 0.0).astype(BF)
    grad = mm_nt(delta, patches_ref[576:2368, :])
    even = is_even("dev")
    keep_ref[...] = jnp.where(even, grad[:, 0:896], grad[:, 896:1792])
    give_ref[...] = jnp.where(even, grad[:, 896:1792], grad[:, 0:896]).astype(BF)


def turn_filters_body(mine_ref, other_ref, w2_ref, wb_ref):
    even = is_even("dev")
    for pair in range(14):
        at = 128 * (pair % 7)
        mine, other = mine_ref[:, at : at + 128].astype(F32), other_ref[:, at : at + 128].astype(F32)
        block = jnp.where(even, mine, other) if pair < 7 else jnp.where(even, other, mine)
        w2_ref[:, 128 * pair : 128 * pair + 128] = block.astype(BF)
        turned = jnp.transpose(block, (1, 0)).astype(BF)
        wb_ref[:, 256 * pair : 256 * pair + 128] = turned[0:64, :]
        if pair < 13:
            wb_ref[:, 256 * pair + 128 : 256 * pair + 256] = turned[64:128, :]


def backward_body(delta_ref, wb_ref, slope_ref, image_ref, low_ref, rim_ref, pooled_ref, keep_ref, give_ref, pd, one):
    for a in range(3):
        for (b, e), value in shifted(delta_ref[128 * a : 128 * a + 128, :].astype(F32)):
            t = 26 - (a * 9 + b * 3 + e)
            pd[128 * t : 128 * t + 128, :] = value.astype(BF)
    back = mm(wb_ref[...], pd[...])
    for r in range(4):
        turned = back if r == 0 else pltpu.roll(back, 256 - 64 * r, 1)
        pooled_ref[:, r, :] = turned[:, 0:64].astype(BF)
    w_in, n_out = rows_of((128, 256)), lanes((128, 256))
    total = jnp.zeros((64, 1024), F32)
    grown = []
    for pair in range(2):
        grow = (w_in == n_out // 2).astype(F32).astype(BF)
        grown.append(split_mm(back[:, 128 * pair : 128 * pair + 128], grow, 3))
    for i in range(2):
        for jp in range(4):
            row = grown[jp // 2][:, 128 * (jp % 2) : 128 * (jp % 2) + 128]
            at = (i * 4 + jp) * 256
            delta = (jnp.concatenate([row, row], axis=1) * slope_ref[:, at : at + 256]).astype(BF)
            cells = patches_one(image_ref, low_ref, rim_ref, i, jp)
            blank = jnp.zeros((32, 256), BF)
            chunks = []
            for s in range(4):
                chunks += [cells[224 * s : min(224 * s + 224, 864), :], blank]
            chunks.append(blank)
            total = total + mm_nt(delta, jnp.concatenate(chunks, axis=0))
    for s in range(4):
        for quarter in range(4):
            for side in range(2):
                at = 256 * s + 128 * side
                one[side, pl.ds(s * 4 + quarter, 16, stride=16), :] = total[16 * quarter : 16 * quarter + 16, at : at + 128]
    even = is_even("dev")
    for c in range(8):
        for side in range(2):
            at = 128 * side
            first, second = one[side, 32 * c : 32 * c + 16, :], one[side, 32 * c + 16 : 32 * c + 32, :]
            keep_ref[16 * c : 16 * c + 16, at : at + 128] = jnp.where(even, first, second)
            give_ref[16 * c : 16 * c + 16, at : at + 128] = jnp.where(even, second, first).astype(BF)


def sum_chip_body(two_ref, other_two_ref, one_ref, other_one_ref, out_ref):
    out_ref[:, 0:896] = (two_ref[...] + other_two_ref[...].astype(F32)).astype(BF)
    out_ref[:, 896:1152] = (one_ref[...] + other_one_ref[...].astype(F32)).astype(BF)


def sum_depth_body(in_ref, act_ref, out_ref, acc):
    total = in_ref[0:16, :].astype(F32)
    for d in range(1, 8):
        total = total + in_ref[16 * d : 16 * d + 16, :].astype(F32)
    act = act_ref[...].astype(F32)
    acc[...] = jnp.zeros(acc.shape, F32)
    for m in range(7):
        acc[1, pl.ds(m, 16, stride=16), :] = total[:, 128 * m : 128 * m + 128]
    for h in range(16):
        for side in range(2):
            at = 16 * h + 8 * side
            acc[0, at : at + 8, :] = act[8 * h : 8 * h + 8, 128 * side : 128 * side + 128]
    out_ref[:, 256:384] = acc[0, 0:256, :].astype(BF)
    out_ref[:, 384:512] = acc[1, 0:256, :].astype(BF)
    one = total[:, 896:1152].astype(BF)
    for h in range(16):
        out_ref[16 * h : 16 * h + 16, 0:256] = one


def sum_height_body(in_ref, out_ref):
    one, two = None, None
    for h in range(16):
        block = in_ref[16 * h : 16 * h + 16, :].astype(F32)
        one = block[:, 0:256] if h == 0 else one + block[:, 0:256]
        two = block[:, 384:512] if h == 0 else two + block[:, 384:512]
    packed = jnp.concatenate([one, two], axis=1).astype(BF)
    for c in range(8):
        out_ref[16 * c : 16 * c + 16, :] = packed


def lay_activation_body(in_ref, act_ref, acc):
    for h in range(16):
        block = in_ref[16 * h : 16 * h + 16, 256:384].astype(F32)
        for r in range(4):
            value = block[8 * (r // 2) : 8 * (r // 2) + 8, :]
            acc[pl.ds(4 * h + r, 8, stride=64), :] = pltpu.roll(value, 64, 1) if r % 2 else value
    act_ref[...] = acc[0:512, :][:, 0:64].astype(BF)


def finish_body(mine_ref, other_ref, one_ref, two_ref, acc):
    even = is_even("dev")
    for c in range(8):
        mine = mine_ref[16 * c : 16 * c + 16, :].astype(F32)
        other = other_ref[16 * c : 16 * c + 16, :].astype(F32)
        first, second = jnp.where(even, mine, other), jnp.where(even, other, mine)
        for part in range(3):
            acc[part, 32 * c : 32 * c + 16, :] = first[:, 128 * part : 128 * part + 128]
            acc[part, 32 * c + 16 : 32 * c + 32, :] = second[:, 128 * part : 128 * part + 128]
    for half in range(2):
        for m in range(7):
            value = acc[2, pl.ds(16 * half + m, 8, stride=32), :] * (1.0 / math.sqrt(CELLS_TWO))
            t = 14 * half + 2 * m
            two_ref[t] = value[:, 0:64]
            if t + 1 < 27:
                two_ref[t + 1] = pltpu.roll(value, 64, 1)[:, 0:64]
    scale = 8.0 / math.sqrt(CELLS_ONE)
    for s in range(4):
        for side in range(2):
            rows = [acc[side, pl.ds(s * 4 + quarter, 16, stride=16), :] for quarter in range(4)]
            turned = jnp.transpose(jnp.concatenate(rows, axis=0), (1, 0)) * scale
            for k in range(4):
                t = 7 * s + 4 * side + k
                if 4 * side + k < 7 and t < 27:
                    one_ref[t] = turned[32 * k : 32 * k + 32, :]


def move(block, axis, step):
    size = lax.axis_size(axis)
    return lax.ppermute(block, axis, [(i, i + step) for i in range(size) if 0 <= i + step < size])


def swap(block, axis, first):
    pairs = [(i, i + 1) for i in range(first, lax.axis_size(axis) - 1, 2)]
    return lax.ppermute(block, axis, pairs + [(j, i) for i, j in pairs])


def exchange(block, axis, groups=None):
    return lax.all_to_all(block, axis, 0, 0, tiled=True, axis_index_groups=groups)


def shards(image, kernel_one, kernel_two, cotangent):
    x = image.reshape(2048, 256)
    k1 = jnp.transpose(kernel_one, (2, 3, 4, 1, 0)).reshape(864, 64)
    k2 = jnp.transpose(kernel_two, (2, 3, 4, 0, 1)).reshape(27, 8, 64)
    cot = cotangent.reshape(512, 64)
    plane, row, corner, packed = call(
        pack_body,
        [shape((512, 256), BF), shape((128, 256), BF), shape((32, 256), BF), shape((128, 1280), BF)],
        [x, k2, cot],
        [
            pltpu.VMEM((2048, 256), BF),
            pltpu.VMEM((27, 8, 64), BF),
            pltpu.VMEM((512, 64), BF),
            pltpu.VMEM((2, 1056, 128), F32),
            pltpu.VMEM((128, 1280), F32),
            pltpu.VMEM((576, 128), F32),
            pltpu.SemaphoreType.DMA((3,)),
        ],
        space=pl.ANY,
        limit=60 * 1024 * 1024,
    )
    plane = move(plane, "dev", 1)
    row = move(row, "ha", 1)
    n_dev, n_ha = lax.axis_size("dev"), lax.axis_size("ha")
    corner = lax.ppermute(
        corner,
        ("dev", "ha"),
        [(d * n_ha + h, (d + 1) * n_ha + h + 1) for d in range(n_dev - 1) for h in range(n_ha - 1)],
    )
    a2 = exchange(packed, "ha")
    own, wt = call(
        turn_image_body,
        [shape((64, 96, 128), BF), shape((64, 864), BF)],
        [x, k1],
        [pltpu.VMEM((2112, 128), F32), pltpu.VMEM((2112, 128), F32)],
        flops=300000000,
    )
    slope, pooled, low, top = call(
        first_layer_body,
        [
            shape((64, 2048), F32),
            shape((64, 256), BF),
            shape((16, 96, 128), BF),
            shape((5, 96, 128), BF),
        ],
        [own, wt, plane, row, corner],
        [pltpu.VMEM((672, 128), F32), pltpu.VMEM((672, 128), F32)],
        flops=400000000,
    )
    other = swap(pooled, "dev", 0)
    (rims,) = call(rims_body, [shape((128, 128), BF)], [pooled, other])
    route = []
    for d in range(n_dev):
        for h in range(d % 2, n_ha - 1, 2):
            route += [(d * n_ha + h, d * n_ha + h + 1), (d * n_ha + h + 1, d * n_ha + h)]
    rims = lax.ppermute(rims, ("dev", "ha"), route)
    a2_other = swap(a2, "dev", 0)
    w2, wb = call(turn_filters_body, [shape((128, 1792), BF), shape((64, 3456), BF)], [a2, a2_other])
    cot_cross = swap(a2[:, 896:1280], "dev", 1)
    rims_core, cot_cross = lax.optimization_barrier((swap(rims, "dev", 0), cot_cross))
    (pair,) = call(widen_body, [shape((128, 512), BF)], [pooled, other, rims, rims_core])
    cross = swap(pair, "dev", 1)
    patches, act, delta = call(
        second_layer_body,
        [shape((2944, 384), BF), shape((128, 256), BF), shape((384, 384), BF)],
        [pair, cross, swap(cross, "dev", 0), w2, a2, a2_other, cot_cross],
        flops=500000000,
    )
    keep_two, give_two = call(
        grad_two_body, [shape((128, 896), F32), shape((128, 896), BF)], [delta, patches], flops=180000000
    )
    grad_pooled, keep_one, give_one = call(
        backward_body,
        [shape((64, 4, 64), BF), shape((128, 256), F32), shape((128, 256), BF)],
        [delta, wb, slope, own, low, top],
        [pltpu.VMEM((3456, 256), BF), pltpu.VMEM((2, 272, 128), F32)],
        flops=400000000,
    )
    (first,) = call(
        sum_chip_body,
        [shape((128, 1152), BF)],
        [keep_two, swap(give_two, "dev", 0), keep_one, swap(give_one, "dev", 0)],
    )
    same_core = [list(range(core, lax.axis_size("dev"), 2)) for core in range(2)]
    (second,) = call(
        sum_depth_body,
        [shape((256, 512), BF)],
        [exchange(first, "dev", same_core), act],
        [pltpu.VMEM((2, 272, 128), F32)],
    )
    second = exchange(second, "ha")
    (third,) = call(sum_height_body, [shape((128, 384), BF)], [second])
    (activation,) = call(lay_activation_body, [shape((512, 64), BF)], [second], [pltpu.VMEM((576, 128), F32)])
    third = exchange(third, "dev", same_core)
    one, two = call(
        finish_body,
        [shape((27, 32, 64), F32), shape((27, 8, 64), F32)],
        [third, swap(third, "dev", 0)],
        [pltpu.VMEM((3, 288, 128), F32)],
    )
    grad_one = jnp.transpose(one.reshape(3, 3, 3, 32, 64), (4, 3, 0, 1, 2))
    grad_two = jnp.transpose(two.reshape(3, 3, 3, 8, 64), (3, 4, 0, 1, 2))
    return (activation.reshape(8, 1, 64, 64), grad_pooled.reshape(64, 1, 4, 64), grad_one, grad_two)


def solution(mesh):
    return jax.shard_map(
        shards,
        mesh=mesh,
        in_specs=(
            P(None, "dev", "ha", None),
            P(),
            P("ha", None, None, None, None),
            P("ha", "dev", None, None),
        ),
        out_specs=(
            P("ha", "dev", None, None),
            P(None, "dev", "ha", None),
            P(),
            P("ha", None, None, None, None),
        ),
        check_vma=False,
    )
```

```python
import math

import jax
import jax.numpy as jnp
from jax import lax
from jax.experimental import pallas as pl
from jax.experimental.pallas import tpu as pltpu
from jax.sharding import PartitionSpec as P

BF = jnp.bfloat16
F32 = jnp.float32
CELLS_ONE = 524288
CELLS_TWO = 65536
VMEM_LIMIT = 32 * 1024 * 1024


def call(body, out_shape, args, scratch=(), flops=1000000, space=pltpu.VMEM, limit=VMEM_LIMIT):
    moved = sum(math.prod(s.shape) * s.dtype.itemsize for s in list(out_shape) + list(args))
    return pl.pallas_call(
        body,
        out_shape=out_shape,
        in_specs=[pl.BlockSpec(memory_space=space)] * len(args),
        out_specs=[pl.BlockSpec(memory_space=pltpu.VMEM)] * len(out_shape),
        scratch_shapes=scratch,
        compiler_params=pltpu.CompilerParams(vmem_limit_bytes=limit),
        cost_estimate=pl.CostEstimate(flops=flops, bytes_accessed=moved, transcendentals=0),
    )(*args)


def shape(dims, dtype):
    return jax.ShapeDtypeStruct(dims, dtype)


def lanes(dims):
    return lax.broadcasted_iota(jnp.int32, dims, len(dims) - 1)


def rows_of(dims):
    return lax.broadcasted_iota(jnp.int32, dims, len(dims) - 2)


def mm(a, b):
    return lax.dot_general(a, b, (((1,), (0,)), ((), ())), preferred_element_type=F32)


def mm_nt(a, b):
    return lax.dot_general(a, b, (((1,), (1,)), ((), ())), preferred_element_type=F32)


def split_mm(a, sel, terms):
    total = None
    for _ in range(terms):
        part = a.astype(BF)
        a = a - part.astype(F32)
        term = mm(part, sel)
        total = term if total is None else total + term
    return total


def pack_body(x_hbm, k_hbm, cot_hbm, plane_ref, row_ref, corner_ref, out_ref, x_ref, k_ref, cot_ref, last, acc, cots, sems):
    copies = []
    for i, (src, dst) in enumerate([(x_hbm, x_ref), (k_hbm, k_ref), (cot_hbm, cot_ref)]):
        copies.append(pltpu.make_async_copy(src, dst, sems.at[i]))
        copies[i].start()
    copies[1].wait()
    even = is_even("dev")
    pieces = []
    for pair in range(7):
        taps = []
        for t in (2 * pair, 2 * pair + 1):
            high = k_ref[t + 14].astype(F32) if t < 13 else jnp.zeros((8, 64), F32)
            taps.append(jnp.where(even, k_ref[t].astype(F32), high))
        pieces.append(jnp.concatenate(taps, axis=1))
    filters = jnp.concatenate(pieces, axis=1)
    for h in range(16):
        acc[8 * h : 8 * h + 8, 0:896] = filters
    copies[2].wait()
    cots[0:512, :] = jnp.concatenate([cot_ref[...].astype(F32), jnp.zeros((512, 64), F32)], axis=1)
    for h in range(16):
        for part in range(3):
            two = []
            for row in (4 * h - 1 + 2 * part, 4 * h + 2 * part):
                two.append(cots[pl.ds(row, 8, stride=64), :] if 0 <= row < 64 else jnp.zeros((8, 128), F32))
            at = 896 + 128 * part
            acc[8 * h : 8 * h + 8, at : at + 128] = two[0] + pltpu.roll(two[1], 64, 1)
    out_ref[...] = acc[...].astype(BF)
    copies[0].wait()
    for c in range(32):
        plane_ref[16 * c : 16 * c + 16, :] = x_ref[64 * c + 48 : 64 * c + 64, :]
    for part in range(128):
        block = x_ref[16 * part : 16 * part + 16, :].astype(F32)[8:16]
        for side in range(2):
            last[side, 8 * part : 8 * part + 8, :] = block[:, 128 * side : 128 * side + 128]
    for side in range(2):
        at = 128 * side
        row_ref[:, at : at + 128] = last[side, pl.ds(7, 128, stride=8), :].astype(BF)
        corner_ref[:, at : at + 128] = last[side, pl.ds(31, 32, stride=32), :].astype(BF)


def parted(value, ev, od, at):
    w_in, n_out = rows_of((256, 256)), lanes((256, 256))
    sel = (w_in == jnp.where(n_out < 128, 2 * n_out, 2 * n_out - 255)).astype(F32).astype(BF)
    both = mm(value, sel)
    ev[at : at + value.shape[0], :] = both[:, :128]
    od[at : at + value.shape[0], :] = both[:, 128:]


def place(out_ref, index, ev, od, start, stride):
    even = ev[pl.ds(start, 32, stride=stride), :]
    odd = od[pl.ds(start, 32, stride=stride), :]
    before = jnp.where(lanes((32, 128)) == 0, 0.0, pltpu.roll(odd, 1, 1))
    out_ref[index, 0:32, :] = before.astype(BF)
    out_ref[index, 32:64, :] = even.astype(BF)
    out_ref[index, 64:96, :] = odd.astype(BF)


def turn_image_body(x_ref, w_ref, own_ref, wt_ref, ev, od):
    for part in range(8):
        parted(x_ref[256 * part : 256 * part + 256, :], ev, od, 256 * part)
    for row in range(64):
        place(own_ref, row, ev, od, row, 64)
    wt_ref[...] = jnp.transpose(w_ref[...].astype(F32), (1, 0)).astype(BF)


def first_layer_body(own_ref, wt_ref, plane_ref, row_ref, corner_ref, slope_ref, pooled_ref, low_ref, top_ref, ev, od):
    for part in range(2):
        parted(plane_ref[256 * part : 256 * part + 256, :], ev, od, 256 * part)
    parted(row_ref[...], ev, od, 512)
    parted(corner_ref[...], ev, od, 640)
    for r in range(16):
        place(low_ref, r, ev, od, r, 16)
    place(top_ref, 0, ev, od, 640, 1)
    for p in range(4):
        place(top_ref, 1 + p, ev, od, 512 + p, 4)
    weights = wt_ref[...]
    sums = [None] * 4
    for i in range(2):
        for jp in range(4):
            pre = mm(weights, patches_one(own_ref, low_ref, top_ref, i, jp))
            sigma = jax.nn.sigmoid(pre)
            at = (i * 4 + jp) * 256
            slope_ref[:, at : at + 256] = sigma * (1.0 + pre * (1.0 - sigma)) * 0.125
            act = pre * sigma
            both = act[:, :128] + act[:, 128:]
            sums[jp] = both if i == 0 else sums[jp] + both
    k_in, k_out = rows_of((256, 128)), lanes((256, 128))
    fold = ((k_in // 2) == k_out).astype(F32).astype(BF)
    halves = []
    for pair in range(2):
        stacked = jnp.concatenate([sums[2 * pair], sums[2 * pair + 1]], axis=1)
        halves.append(split_mm(stacked, fold, 3) * 0.125)
    pooled = jnp.concatenate(halves, axis=1)
    pooled_ref[...] = pooled.astype(BF)


def patches_one(own_ref, low_ref, top_ref, i, jp):
    def block(a, b):
        if b == 0:
            return top_ref[a]
        return low_ref[b - 1] if a == 0 else own_ref[(a - 1) * 16 + b - 1]

    columns = []
    for j in (2 * jp, 2 * jp + 1):
        columns.append(jnp.concatenate([block(2 * i + a, 2 * j + b) for a in range(3) for b in range(3)], axis=0))
    return jnp.concatenate(columns, axis=1)


def is_even(axis):
    return lax.axis_index(axis) % 2 == 0


def shifted(ext):
    width = ext.shape[1]
    kept = width - 128
    column = lanes(ext.shape) & 63
    for e in range(3):
        if e == 0:
            moved = jnp.where(column == 0, 0.0, pltpu.roll(ext, 1, 1))
        elif e == 2:
            moved = jnp.where(column == 63, 0.0, pltpu.roll(ext, width - 1, 1))
        else:
            moved = ext
        yield (0, e), moved[:, 0:kept]
        yield (1, e), pltpu.roll(moved, width - 64, 1)[:, 0:kept]
        yield (2, e), moved[:, 128:width]


def rims_body(own_ref, other_ref, out_ref):
    bottom = is_even("ha") == is_even("dev")
    for k, ref in enumerate((own_ref, other_ref)):
        value = ref[...].astype(F32)
        out_ref[64 * k : 64 * k + 64, :] = jnp.where(bottom, value[:, 128:256], value[:, 0:128]).astype(BF)


def widen_body(own_ref, other_ref, mine_ref, core_ref, out_ref):
    swapped = is_even("ha") == is_even("dev")
    mine, core = mine_ref[...].astype(F32), core_ref[...].astype(F32)
    for k, ref in enumerate((own_ref, other_ref)):
        here, there = mine[64 * k : 64 * k + 64], core[64 - 64 * k : 128 - 64 * k]
        out_ref[64 * k : 64 * k + 64, 0:128] = jnp.where(swapped, there, here).astype(BF)
        out_ref[64 * k : 64 * k + 64, 128:384] = ref[...]
        out_ref[64 * k : 64 * k + 64, 384:512] = jnp.where(swapped, here, there).astype(BF)


def second_layer_body(pair_ref, cross_ref, core_ref, w2_ref, a2_ref, other_ref, cot_ref, patches_ref, act_ref, delta_ref):
    even = is_even("dev")

    def planes(ref):
        return ref[0:64, 0:512].astype(F32), ref[64:128, 0:512].astype(F32)

    own, other = planes(pair_ref)
    near, far = planes(cross_ref)
    beyond = core_ref[0:64, 0:512].astype(F32)
    ordered = (
        jnp.where(even, far, beyond),
        jnp.where(even, near, other),
        own,
        jnp.where(even, other, near),
        jnp.where(even, beyond, far),
    )
    for a, plane in enumerate(ordered):
        for (b, e), value in shifted(plane):
            t = a * 9 + b * 3 + e
            patches_ref[64 * t : 64 * t + 64, :] = value.astype(BF)
    patches_ref[2880:2944, :] = jnp.zeros((64, 384), BF)
    cot_cross, cot_core = cot_ref[...].astype(F32), other_ref[:, 896:1280].astype(F32)
    cots = (
        jnp.where(even, cot_cross, cot_core),
        a2_ref[:, 896:1280].astype(F32),
        jnp.where(even, cot_core, cot_cross),
    )
    for p in range(3):
        pre = mm(w2_ref[...], patches_ref[576 * p : 576 * p + 1792, :])
        sigma = jax.nn.sigmoid(pre)
        if p == 1:
            act_ref[...] = pltpu.roll(pre * sigma, 320, 1)[:, 0:256].astype(BF)
        slope = sigma * (1.0 + pre * (1.0 - sigma))
        delta_ref[128 * p : 128 * p + 128, :] = (cots[p] * slope).astype(BF)


def grad_two_body(delta_ref, patches_ref, keep_ref, give_ref):
    r, o = rows_of((128, 128)), lanes((128, 128))
    order = (o == (r % 16) * 8 + r // 16).astype(F32).astype(BF)
    cell = lanes((128, 384))
    mine = (cell >= 64) & (cell < 320)
    delta = jnp.where(mine, mm(order, delta_ref[128:256, :]), 0.0).astype(BF)
    grad = mm_nt(delta, patches_ref[576:2368, :])
    even = is_even("dev")
    keep_ref[...] = jnp.where(even, grad[:, 0:896], grad[:, 896:1792])
    give_ref[...] = jnp.where(even, grad[:, 896:1792], grad[:, 0:896]).astype(BF)


def turn_filters_body(mine_ref, other_ref, w2_ref, wb_ref):
    even = is_even("dev")
    for pair in range(14):
        at = 128 * (pair % 7)
        mine, other = mine_ref[:, at : at + 128].astype(F32), other_ref[:, at : at + 128].astype(F32)
        block = jnp.where(even, mine, other) if pair < 7 else jnp.where(even, other, mine)
        w2_ref[:, 128 * pair : 128 * pair + 128] = block.astype(BF)
        turned = jnp.transpose(block, (1, 0)).astype(BF)
        wb_ref[:, 256 * pair : 256 * pair + 128] = turned[0:64, :]
        if pair < 13:
            wb_ref[:, 256 * pair + 128 : 256 * pair + 256] = turned[64:128, :]


def backward_body(delta_ref, wb_ref, slope_ref, image_ref, low_ref, rim_ref, pooled_ref, keep_ref, give_ref, pd, one):
    for a in range(3):
        for (b, e), value in shifted(delta_ref[128 * a : 128 * a + 128, :].astype(F32)):
            t = 26 - (a * 9 + b * 3 + e)
            pd[128 * t : 128 * t + 128, :] = value.astype(BF)
    back = mm(wb_ref[...], pd[...])
    for r in range(4):
        turned = back if r == 0 else pltpu.roll(back, 256 - 64 * r, 1)
        pooled_ref[:, r, :] = turned[:, 0:64].astype(BF)
    w_in, n_out = rows_of((128, 256)), lanes((128, 256))
    total = jnp.zeros((64, 1024), F32)
    grown = []
    for pair in range(2):
        grow = (w_in == n_out // 2).astype(F32).astype(BF)
        grown.append(split_mm(back[:, 128 * pair : 128 * pair + 128], grow, 3))
    for i in range(2):
        for jp in range(4):
            row = grown[jp // 2][:, 128 * (jp % 2) : 128 * (jp % 2) + 128]
            at = (i * 4 + jp) * 256
            delta = (jnp.concatenate([row, row], axis=1) * slope_ref[:, at : at + 256]).astype(BF)
            cells = patches_one(image_ref, low_ref, rim_ref, i, jp)
            blank = jnp.zeros((32, 256), BF)
            chunks = []
            for s in range(4):
                chunks += [cells[224 * s : min(224 * s + 224, 864), :], blank]
            chunks.append(blank)
            total = total + mm_nt(delta, jnp.concatenate(chunks, axis=0))
    for s in range(4):
        for quarter in range(4):
            for side in range(2):
                at = 256 * s + 128 * side
                one[side, pl.ds(s * 4 + quarter, 16, stride=16), :] = total[16 * quarter : 16 * quarter + 16, at : at + 128]
    even = is_even("dev")
    for c in range(8):
        for side in range(2):
            at = 128 * side
            first, second = one[side, 32 * c : 32 * c + 16, :], one[side, 32 * c + 16 : 32 * c + 32, :]
            keep_ref[16 * c : 16 * c + 16, at : at + 128] = jnp.where(even, first, second)
            give_ref[16 * c : 16 * c + 16, at : at + 128] = jnp.where(even, second, first).astype(BF)


def sum_chip_body(two_ref, other_two_ref, one_ref, other_one_ref, out_ref):
    out_ref[:, 0:896] = (two_ref[...] + other_two_ref[...].astype(F32)).astype(BF)
    out_ref[:, 896:1152] = (one_ref[...] + other_one_ref[...].astype(F32)).astype(BF)


def sum_depth_body(in_ref, act_ref, out_ref, acc):
    total = in_ref[0:16, :].astype(F32)
    for d in range(1, 8):
        total = total + in_ref[16 * d : 16 * d + 16, :].astype(F32)
    act = act_ref[...].astype(F32)
    acc[...] = jnp.zeros(acc.shape, F32)
    for m in range(7):
        acc[pl.ds(48 + m, 16, stride=56), :] = total[:, 128 * m : 128 * m + 128]
    for h in range(16):
        for side in range(2):
            at = 56 * h + 16 * side
            acc[at : at + 16, :] = total[:, 896 + 128 * side : 1024 + 128 * side]
            at = 56 * h + 32 + 8 * side
            acc[at : at + 8, :] = act[8 * h : 8 * h + 8, 128 * side : 128 * side + 128]
    out_ref[...] = acc[0:896, :].astype(BF)


def sum_height_body(in_ref, out_ref):
    value = in_ref[...].astype(F32)
    total = value[0:56]
    for h in range(1, 16):
        total = total + value[56 * h : 56 * h + 56]
    two = jnp.concatenate([total[48:56], jnp.zeros((8, 128), F32)], axis=0)
    packed = jnp.concatenate([total[0:16], total[16:32], two], axis=1).astype(BF)
    for c in range(8):
        out_ref[16 * c : 16 * c + 16, :] = packed


def lay_activation_body(in_ref, act_ref, acc):
    rows = in_ref[...].astype(F32)
    for h in range(16):
        for r in range(4):
            at = 56 * h + 32 + 8 * (r // 2)
            value = rows[at : at + 8]
            acc[pl.ds(4 * h + r, 8, stride=64), :] = pltpu.roll(value, 64, 1) if r % 2 else value
    act_ref[...] = acc[0:512, :][:, 0:64].astype(BF)


def finish_body(mine_ref, other_ref, one_ref, two_ref, acc):
    even = is_even("dev")
    for c in range(8):
        mine = mine_ref[16 * c : 16 * c + 16, :].astype(F32)
        other = other_ref[16 * c : 16 * c + 16, :].astype(F32)
        first, second = jnp.where(even, mine, other), jnp.where(even, other, mine)
        for part in range(3):
            acc[part, 32 * c : 32 * c + 16, :] = first[:, 128 * part : 128 * part + 128]
            acc[part, 32 * c + 16 : 32 * c + 32, :] = second[:, 128 * part : 128 * part + 128]
    for half in range(2):
        for m in range(7):
            value = acc[2, pl.ds(16 * half + m, 8, stride=32), :] * (1.0 / math.sqrt(CELLS_TWO))
            t = 14 * half + 2 * m
            two_ref[t] = value[:, 0:64]
            if t + 1 < 27:
                two_ref[t + 1] = pltpu.roll(value, 64, 1)[:, 0:64]
    scale = 8.0 / math.sqrt(CELLS_ONE)
    for s in range(4):
        for side in range(2):
            rows = [acc[side, pl.ds(s * 4 + quarter, 16, stride=16), :] for quarter in range(4)]
            turned = jnp.transpose(jnp.concatenate(rows, axis=0), (1, 0)) * scale
            for k in range(4):
                t = 7 * s + 4 * side + k
                if 4 * side + k < 7 and t < 27:
                    one_ref[t] = turned[32 * k : 32 * k + 32, :]


def move(block, axis, step):
    size = lax.axis_size(axis)
    return lax.ppermute(block, axis, [(i, i + step) for i in range(size) if 0 <= i + step < size])


def swap(block, axis, first):
    pairs = [(i, i + 1) for i in range(first, lax.axis_size(axis) - 1, 2)]
    return lax.ppermute(block, axis, pairs + [(j, i) for i, j in pairs])


def exchange(block, axis, groups=None):
    return lax.all_to_all(block, axis, 0, 0, tiled=True, axis_index_groups=groups)


def shards(image, kernel_one, kernel_two, cotangent):
    x = image.reshape(2048, 256)
    k1 = jnp.transpose(kernel_one, (2, 3, 4, 1, 0)).reshape(864, 64)
    k2 = jnp.transpose(kernel_two, (2, 3, 4, 0, 1)).reshape(27, 8, 64)
    cot = cotangent.reshape(512, 64)
    plane, row, corner, packed = call(
        pack_body,
        [shape((512, 256), BF), shape((128, 256), BF), shape((32, 256), BF), shape((128, 1280), BF)],
        [x, k2, cot],
        [
            pltpu.VMEM((2048, 256), BF),
            pltpu.VMEM((27, 8, 64), BF),
            pltpu.VMEM((512, 64), BF),
            pltpu.VMEM((2, 1056, 128), F32),
            pltpu.VMEM((128, 1280), F32),
            pltpu.VMEM((576, 128), F32),
            pltpu.SemaphoreType.DMA((3,)),
        ],
        space=pl.ANY,
        limit=60 * 1024 * 1024,
    )
    plane = move(plane, "dev", 1)
    row = move(row, "ha", 1)
    n_dev, n_ha = lax.axis_size("dev"), lax.axis_size("ha")
    corner = lax.ppermute(
        corner,
        ("dev", "ha"),
        [(d * n_ha + h, (d + 1) * n_ha + h + 1) for d in range(n_dev - 1) for h in range(n_ha - 1)],
    )
    a2 = exchange(packed, "ha")
    own, wt = call(
        turn_image_body,
        [shape((64, 96, 128), BF), shape((64, 864), BF)],
        [x, k1],
        [pltpu.VMEM((2112, 128), F32), pltpu.VMEM((2112, 128), F32)],
        flops=300000000,
    )
    slope, pooled, low, top = call(
        first_layer_body,
        [
            shape((64, 2048), F32),
            shape((64, 256), BF),
            shape((16, 96, 128), BF),
            shape((5, 96, 128), BF),
        ],
        [own, wt, plane, row, corner],
        [pltpu.VMEM((672, 128), F32), pltpu.VMEM((672, 128), F32)],
        flops=400000000,
    )
    other = swap(pooled, "dev", 0)
    (rims,) = call(rims_body, [shape((128, 128), BF)], [pooled, other])
    route = []
    for d in range(n_dev):
        for h in range(d % 2, n_ha - 1, 2):
            route += [(d * n_ha + h, d * n_ha + h + 1), (d * n_ha + h + 1, d * n_ha + h)]
    rims = lax.ppermute(rims, ("dev", "ha"), route)
    a2_other = swap(a2, "dev", 0)
    w2, wb = call(turn_filters_body, [shape((128, 1792), BF), shape((64, 3456), BF)], [a2, a2_other])
    cot_cross = swap(a2[:, 896:1280], "dev", 1)
    rims_core, cot_cross = lax.optimization_barrier((swap(rims, "dev", 0), cot_cross))
    (pair,) = call(widen_body, [shape((128, 512), BF)], [pooled, other, rims, rims_core])
    cross = swap(pair, "dev", 1)
    patches, act, delta = call(
        second_layer_body,
        [shape((2944, 384), BF), shape((128, 256), BF), shape((384, 384), BF)],
        [pair, cross, swap(cross, "dev", 0), w2, a2, a2_other, cot_cross],
        flops=500000000,
    )
    keep_two, give_two = call(
        grad_two_body, [shape((128, 896), F32), shape((128, 896), BF)], [delta, patches], flops=180000000
    )
    grad_pooled, keep_one, give_one = call(
        backward_body,
        [shape((64, 4, 64), BF), shape((128, 256), F32), shape((128, 256), BF)],
        [delta, wb, slope, own, low, top],
        [pltpu.VMEM((3456, 256), BF), pltpu.VMEM((2, 272, 128), F32)],
        flops=400000000,
    )
    (first,) = call(
        sum_chip_body,
        [shape((128, 1152), BF)],
        [keep_two, swap(give_two, "dev", 0), keep_one, swap(give_one, "dev", 0)],
    )
    same_core = [list(range(core, lax.axis_size("dev"), 2)) for core in range(2)]
    (second,) = call(
        sum_depth_body,
        [shape((896, 128), BF)],
        [exchange(first, "dev", same_core), act],
        [pltpu.VMEM((960, 128), F32)],
    )
    second = exchange(second, "ha")
    (third,) = call(sum_height_body, [shape((128, 384), BF)], [second])
    (activation,) = call(lay_activation_body, [shape((512, 64), BF)], [second], [pltpu.VMEM((576, 128), F32)])
    third = exchange(third, "dev", same_core)
    one, two = call(
        finish_body,
        [shape((27, 32, 64), F32), shape((27, 8, 64), F32)],
        [third, swap(third, "dev", 0)],
        [pltpu.VMEM((3, 288, 128), F32)],
    )
    grad_one = jnp.transpose(one.reshape(3, 3, 3, 32, 64), (4, 3, 0, 1, 2))
    grad_two = jnp.transpose(two.reshape(3, 3, 3, 8, 64), (3, 4, 0, 1, 2))
    return (activation.reshape(8, 1, 64, 64), grad_pooled.reshape(64, 1, 4, 64), grad_one, grad_two)


def solution(mesh):
    return jax.shard_map(
        shards,
        mesh=mesh,
        in_specs=(
            P(None, "dev", "ha", None),
            P(),
            P("ha", None, None, None, None),
            P("ha", "dev", None, None),
        ),
        out_specs=(
            P("ha", "dev", None, None),
            P(None, "dev", "ha", None),
            P(),
            P("ha", None, None, None, None),
        ),
        check_vma=False,
    )
```

```python
import math

import jax
import jax.numpy as jnp
from jax import lax
from jax.experimental import pallas as pl
from jax.experimental.pallas import tpu as pltpu
from jax.sharding import PartitionSpec as P

BF = jnp.bfloat16
F32 = jnp.float32
CELLS_ONE = 524288
CELLS_TWO = 65536
VMEM_LIMIT = 32 * 1024 * 1024


def call(body, out_shape, args, scratch=(), flops=1000000, space=pltpu.VMEM, limit=VMEM_LIMIT):
    moved = sum(math.prod(s.shape) * s.dtype.itemsize for s in list(out_shape) + list(args))
    return pl.pallas_call(
        body,
        out_shape=out_shape,
        in_specs=[pl.BlockSpec(memory_space=space)] * len(args),
        out_specs=[pl.BlockSpec(memory_space=pltpu.VMEM)] * len(out_shape),
        scratch_shapes=scratch,
        compiler_params=pltpu.CompilerParams(vmem_limit_bytes=limit),
        cost_estimate=pl.CostEstimate(flops=flops, bytes_accessed=moved, transcendentals=0),
    )(*args)


def shape(dims, dtype):
    return jax.ShapeDtypeStruct(dims, dtype)


def lanes(dims):
    return lax.broadcasted_iota(jnp.int32, dims, len(dims) - 1)


def rows_of(dims):
    return lax.broadcasted_iota(jnp.int32, dims, len(dims) - 2)


def mm(a, b):
    return lax.dot_general(a, b, (((1,), (0,)), ((), ())), preferred_element_type=F32)


def mm_nt(a, b):
    return lax.dot_general(a, b, (((1,), (1,)), ((), ())), preferred_element_type=F32)


def split_mm(a, sel, terms):
    total = None
    for _ in range(terms):
        part = a.astype(BF)
        a = a - part.astype(F32)
        term = mm(part, sel)
        total = term if total is None else total + term
    return total


def pack_body(x_hbm, k_hbm, cot_hbm, plane_ref, row_ref, corner_ref, out_ref, x_ref, k_ref, cot_ref, last, acc, cots, sems):
    copies = []
    for i, (src, dst) in enumerate([(x_hbm, x_ref), (k_hbm, k_ref), (cot_hbm, cot_ref)]):
        copies.append(pltpu.make_async_copy(src, dst, sems.at[i]))
        copies[i].start()
    copies[1].wait()
    even = is_even("dev")
    pieces = []
    for pair in range(7):
        taps = []
        for t in (2 * pair, 2 * pair + 1):
            high = k_ref[t + 14].astype(F32) if t < 13 else jnp.zeros((8, 64), F32)
            taps.append(jnp.where(even, k_ref[t].astype(F32), high))
        pieces.append(jnp.concatenate(taps, axis=1))
    filters = jnp.concatenate(pieces, axis=1)
    for h in range(16):
        acc[8 * h : 8 * h + 8, 0:896] = filters
    copies[2].wait()
    cots[0:512, :] = jnp.concatenate([cot_ref[...].astype(F32), jnp.zeros((512, 64), F32)], axis=1)
    for h in range(16):
        for part in range(3):
            two = []
            for row in (4 * h - 1 + 2 * part, 4 * h + 2 * part):
                two.append(cots[pl.ds(row, 8, stride=64), :] if 0 <= row < 64 else jnp.zeros((8, 128), F32))
            at = 896 + 128 * part
            acc[8 * h : 8 * h + 8, at : at + 128] = two[0] + pltpu.roll(two[1], 64, 1)
    out_ref[...] = acc[...].astype(BF)
    copies[0].wait()
    for c in range(32):
        plane_ref[16 * c : 16 * c + 16, :] = x_ref[64 * c + 48 : 64 * c + 64, :]
    for part in range(128):
        block = x_ref[16 * part : 16 * part + 16, :].astype(F32)[8:16]
        for side in range(2):
            last[side, 8 * part : 8 * part + 8, :] = block[:, 128 * side : 128 * side + 128]
    for side in range(2):
        at = 128 * side
        row_ref[:, at : at + 128] = last[side, pl.ds(7, 128, stride=8), :].astype(BF)
        corner_ref[:, at : at + 128] = last[side, pl.ds(31, 32, stride=32), :].astype(BF)


def parted(value, ev, od, at):
    w_in, n_out = rows_of((256, 256)), lanes((256, 256))
    sel = (w_in == jnp.where(n_out < 128, 2 * n_out, 2 * n_out - 255)).astype(F32).astype(BF)
    both = mm(value, sel)
    ev[at : at + value.shape[0], :] = both[:, :128]
    od[at : at + value.shape[0], :] = both[:, 128:]


def place(out_ref, index, ev, od, start, stride):
    even = ev[pl.ds(start, 32, stride=stride), :]
    odd = od[pl.ds(start, 32, stride=stride), :]
    before = jnp.where(lanes((32, 128)) == 0, 0.0, pltpu.roll(odd, 1, 1))
    out_ref[index, 0:32, :] = before.astype(BF)
    out_ref[index, 32:64, :] = even.astype(BF)
    out_ref[index, 64:96, :] = odd.astype(BF)


def turn_image_body(x_ref, w_ref, own_ref, wt_ref, ev, od):
    for part in range(8):
        parted(x_ref[256 * part : 256 * part + 256, :], ev, od, 256 * part)
    for row in range(64):
        place(own_ref, row, ev, od, row, 64)
    wt_ref[...] = jnp.transpose(w_ref[...].astype(F32), (1, 0)).astype(BF)


def first_layer_body(own_ref, wt_ref, plane_ref, row_ref, corner_ref, slope_ref, pooled_ref, low_ref, top_ref, ev, od):
    for part in range(2):
        parted(plane_ref[256 * part : 256 * part + 256, :], ev, od, 256 * part)
    parted(row_ref[...], ev, od, 512)
    parted(corner_ref[...], ev, od, 640)
    for r in range(16):
        place(low_ref, r, ev, od, r, 16)
    place(top_ref, 0, ev, od, 640, 1)
    for p in range(4):
        place(top_ref, 1 + p, ev, od, 512 + p, 4)
    weights = wt_ref[...]
    sums = [None] * 4
    for i in range(2):
        for jp in range(4):
            pre = mm(weights, patches_one(own_ref, low_ref, top_ref, i, jp))
            sigma = jax.nn.sigmoid(pre)
            at = (i * 4 + jp) * 256
            slope_ref[:, at : at + 256] = sigma * (1.0 + pre * (1.0 - sigma)) * 0.125
            act = pre * sigma
            both = act[:, :128] + act[:, 128:]
            sums[jp] = both if i == 0 else sums[jp] + both
    k_in, k_out = rows_of((256, 128)), lanes((256, 128))
    fold = ((k_in // 2) == k_out).astype(F32).astype(BF)
    halves = []
    for pair in range(2):
        stacked = jnp.concatenate([sums[2 * pair], sums[2 * pair + 1]], axis=1)
        halves.append(split_mm(stacked, fold, 3) * 0.125)
    pooled = jnp.concatenate(halves, axis=1)
    pooled_ref[...] = pooled.astype(BF)


def patches_one(own_ref, low_ref, top_ref, i, jp):
    def block(a, b):
        if b == 0:
            return top_ref[a]
        return low_ref[b - 1] if a == 0 else own_ref[(a - 1) * 16 + b - 1]

    columns = []
    for j in (2 * jp, 2 * jp + 1):
        columns.append(jnp.concatenate([block(2 * i + a, 2 * j + b) for a in range(3) for b in range(3)], axis=0))
    return jnp.concatenate(columns, axis=1)


def is_even(axis):
    return lax.axis_index(axis) % 2 == 0


def shifted(ext):
    width = ext.shape[1]
    kept = width - 128
    column = lanes(ext.shape) & 63
    for e in range(3):
        if e == 0:
            moved = jnp.where(column == 0, 0.0, pltpu.roll(ext, 1, 1))
        elif e == 2:
            moved = jnp.where(column == 63, 0.0, pltpu.roll(ext, width - 1, 1))
        else:
            moved = ext
        yield (0, e), moved[:, 0:kept]
        yield (1, e), pltpu.roll(moved, width - 64, 1)[:, 0:kept]
        yield (2, e), moved[:, 128:width]


def rims_body(own_ref, other_ref, out_ref):
    bottom = is_even("ha") == is_even("dev")
    for k, ref in enumerate((own_ref, other_ref)):
        value = ref[...].astype(F32)
        out_ref[64 * k : 64 * k + 64, :] = jnp.where(bottom, value[:, 128:256], value[:, 0:128]).astype(BF)


def widen_body(own_ref, other_ref, mine_ref, core_ref, out_ref):
    swapped = is_even("ha") == is_even("dev")
    mine, core = mine_ref[...].astype(F32), core_ref[...].astype(F32)
    for k, ref in enumerate((own_ref, other_ref)):
        here, there = mine[64 * k : 64 * k + 64], core[64 - 64 * k : 128 - 64 * k]
        out_ref[64 * k : 64 * k + 64, 0:128] = jnp.where(swapped, there, here).astype(BF)
        out_ref[64 * k : 64 * k + 64, 128:384] = ref[...]
        out_ref[64 * k : 64 * k + 64, 384:512] = jnp.where(swapped, here, there).astype(BF)


def second_layer_body(pair_ref, cross_ref, core_ref, w2_ref, a2_ref, other_ref, cot_ref, patches_ref, act_ref, delta_ref):
    even = is_even("dev")

    def planes(ref):
        return ref[0:64, 0:512].astype(F32), ref[64:128, 0:512].astype(F32)

    own, other = planes(pair_ref)
    near, far = planes(cross_ref)
    beyond = core_ref[0:64, 0:512].astype(F32)
    ordered = (
        jnp.where(even, far, beyond),
        jnp.where(even, near, other),
        own,
        jnp.where(even, other, near),
        jnp.where(even, beyond, far),
    )
    for a, plane in enumerate(ordered):
        for (b, e), value in shifted(plane):
            t = a * 9 + b * 3 + e
            patches_ref[64 * t : 64 * t + 64, :] = value.astype(BF)
    patches_ref[2880:2944, :] = jnp.zeros((64, 384), BF)
    cot_cross, cot_core = cot_ref[...].astype(F32), other_ref[:, 896:1280].astype(F32)
    cots = (
        jnp.where(even, cot_cross, cot_core),
        a2_ref[:, 896:1280].astype(F32),
        jnp.where(even, cot_core, cot_cross),
    )
    for p in range(3):
        pre = mm(w2_ref[...], patches_ref[576 * p : 576 * p + 1792, :])
        sigma = jax.nn.sigmoid(pre)
        if p == 1:
            act_ref[...] = pltpu.roll(pre * sigma, 320, 1)[:, 0:256].astype(BF)
        slope = sigma * (1.0 + pre * (1.0 - sigma))
        delta_ref[128 * p : 128 * p + 128, :] = (cots[p] * slope).astype(BF)


def grad_two_body(delta_ref, patches_ref, keep_ref, give_ref):
    r, o = rows_of((128, 128)), lanes((128, 128))
    order = (o == (r % 16) * 8 + r // 16).astype(F32).astype(BF)
    cell = lanes((128, 384))
    mine = (cell >= 64) & (cell < 320)
    delta = jnp.where(mine, mm(order, delta_ref[128:256, :]), 0.0).astype(BF)
    grad = mm_nt(delta, patches_ref[576:2368, :])
    even = is_even("dev")
    keep_ref[...] = jnp.where(even, grad[:, 0:896], grad[:, 896:1792])
    give_ref[...] = jnp.where(even, grad[:, 896:1792], grad[:, 0:896]).astype(BF)


def turn_filters_body(mine_ref, other_ref, w2_ref, wb_ref):
    even = is_even("dev")
    for pair in range(14):
        at = 128 * (pair % 7)
        mine, other = mine_ref[:, at : at + 128].astype(F32), other_ref[:, at : at + 128].astype(F32)
        block = jnp.where(even, mine, other) if pair < 7 else jnp.where(even, other, mine)
        w2_ref[:, 128 * pair : 128 * pair + 128] = block.astype(BF)
        turned = jnp.transpose(block, (1, 0)).astype(BF)
        wb_ref[:, 256 * pair : 256 * pair + 128] = turned[0:64, :]
        if pair < 13:
            wb_ref[:, 256 * pair + 128 : 256 * pair + 256] = turned[64:128, :]


def backward_body(delta_ref, wb_ref, slope_ref, image_ref, low_ref, rim_ref, pooled_ref, keep_ref, give_ref, pd, one):
    for a in range(3):
        for (b, e), value in shifted(delta_ref[128 * a : 128 * a + 128, :].astype(F32)):
            t = 26 - (a * 9 + b * 3 + e)
            pd[128 * t : 128 * t + 128, :] = value.astype(BF)
    back = mm(wb_ref[...], pd[...])
    for r in range(4):
        turned = back if r == 0 else pltpu.roll(back, 256 - 64 * r, 1)
        pooled_ref[:, r, :] = turned[:, 0:64].astype(BF)
    w_in, n_out = rows_of((128, 256)), lanes((128, 256))
    total = jnp.zeros((64, 1024), F32)
    grown = []
    for pair in range(2):
        grow = (w_in == n_out // 2).astype(F32).astype(BF)
        grown.append(split_mm(back[:, 128 * pair : 128 * pair + 128], grow, 3))
    for i in range(2):
        for jp in range(4):
            row = grown[jp // 2][:, 128 * (jp % 2) : 128 * (jp % 2) + 128]
            at = (i * 4 + jp) * 256
            delta = (jnp.concatenate([row, row], axis=1) * slope_ref[:, at : at + 256]).astype(BF)
            cells = patches_one(image_ref, low_ref, rim_ref, i, jp)
            blank = jnp.zeros((32, 256), BF)
            chunks = []
            for s in range(4):
                chunks += [cells[224 * s : min(224 * s + 224, 864), :], blank]
            chunks.append(blank)
            total = total + mm_nt(delta, jnp.concatenate(chunks, axis=0))
    for s in range(4):
        for quarter in range(4):
            for side in range(2):
                at = 256 * s + 128 * side
                one[side, pl.ds(s * 4 + quarter, 16, stride=16), :] = total[16 * quarter : 16 * quarter + 16, at : at + 128]
    even = is_even("dev")
    for c in range(8):
        for side in range(2):
            at = 128 * side
            first, second = one[side, 32 * c : 32 * c + 16, :], one[side, 32 * c + 16 : 32 * c + 32, :]
            keep_ref[16 * c : 16 * c + 16, at : at + 128] = jnp.where(even, first, second)
            give_ref[16 * c : 16 * c + 16, at : at + 128] = jnp.where(even, second, first).astype(BF)


def sum_chip_body(two_ref, other_two_ref, one_ref, other_one_ref, out_ref):
    out_ref[:, 0:896] = (two_ref[...] + other_two_ref[...].astype(F32)).astype(BF)
    out_ref[:, 896:1152] = (one_ref[...] + other_one_ref[...].astype(F32)).astype(BF)


def sum_depth_body(in_ref, act_ref, out_ref, acc):
    total = in_ref[0:16, :].astype(F32)
    for d in range(1, 8):
        total = total + in_ref[16 * d : 16 * d + 16, :].astype(F32)
    act = act_ref[...].astype(F32)
    acc[...] = jnp.zeros(acc.shape, F32)
    for m in range(7):
        acc[pl.ds(48 + m, 16, stride=56), :] = total[:, 128 * m : 128 * m + 128]
    for h in range(16):
        for side in range(2):
            at = 56 * h + 16 * side
            acc[at : at + 16, :] = total[:, 896 + 128 * side : 1024 + 128 * side]
            at = 56 * h + 32 + 8 * side
            acc[at : at + 8, :] = act[8 * h : 8 * h + 8, 128 * side : 128 * side + 128]
    out_ref[...] = acc[0:896, :].astype(BF)


def sum_height_body(in_ref, out_ref):
    value = in_ref[...].astype(F32)
    total = value[0:56]
    for h in range(1, 16):
        total = total + value[56 * h : 56 * h + 56]
    packed = jnp.concatenate([total[0:32], total[48:56]], axis=0)
    out_ref[...] = jnp.concatenate([packed] * 8, axis=0).astype(BF)


def lay_activation_body(in_ref, act_ref, acc):
    rows = in_ref[...].astype(F32)
    for h in range(16):
        for r in range(4):
            at = 56 * h + 32 + 8 * (r // 2)
            value = rows[at : at + 8]
            acc[pl.ds(4 * h + r, 8, stride=64), :] = pltpu.roll(value, 64, 1) if r % 2 else value
    act_ref[...] = acc[0:512, :][:, 0:64].astype(BF)


def finish_body(mine_ref, other_ref, one_ref, two_ref, acc):
    even = is_even("dev")
    mine, other = mine_ref[...].astype(F32), other_ref[...].astype(F32)
    first, second = jnp.where(even, mine, other), jnp.where(even, other, mine)
    for c in range(8):
        for part, count in enumerate((16, 16, 8)):
            at = 40 * c + 16 * part
            acc[part, 32 * c : 32 * c + count, :] = first[at : at + count]
            acc[part, 32 * c + 16 : 32 * c + 16 + count, :] = second[at : at + count]
    for half in range(2):
        for m in range(7):
            value = acc[2, pl.ds(16 * half + m, 8, stride=32), :] * (1.0 / math.sqrt(CELLS_TWO))
            t = 14 * half + 2 * m
            two_ref[t] = value[:, 0:64]
            if t + 1 < 27:
                two_ref[t + 1] = pltpu.roll(value, 64, 1)[:, 0:64]
    scale = 8.0 / math.sqrt(CELLS_ONE)
    for s in range(4):
        for side in range(2):
            rows = [acc[side, pl.ds(s * 4 + quarter, 16, stride=16), :] for quarter in range(4)]
            turned = jnp.transpose(jnp.concatenate(rows, axis=0), (1, 0)) * scale
            for k in range(4):
                t = 7 * s + 4 * side + k
                if 4 * side + k < 7 and t < 27:
                    one_ref[t] = turned[32 * k : 32 * k + 32, :]


def move(block, axis, step):
    size = lax.axis_size(axis)
    return lax.ppermute(block, axis, [(i, i + step) for i in range(size) if 0 <= i + step < size])


def swap(block, axis, first):
    pairs = [(i, i + 1) for i in range(first, lax.axis_size(axis) - 1, 2)]
    return lax.ppermute(block, axis, pairs + [(j, i) for i, j in pairs])


def exchange(block, axis, groups=None):
    return lax.all_to_all(block, axis, 0, 0, tiled=True, axis_index_groups=groups)


def shards(image, kernel_one, kernel_two, cotangent):
    x = image.reshape(2048, 256)
    k1 = jnp.transpose(kernel_one, (2, 3, 4, 1, 0)).reshape(864, 64)
    k2 = jnp.transpose(kernel_two, (2, 3, 4, 0, 1)).reshape(27, 8, 64)
    cot = cotangent.reshape(512, 64)
    plane, row, corner, packed = call(
        pack_body,
        [shape((512, 256), BF), shape((128, 256), BF), shape((32, 256), BF), shape((128, 1280), BF)],
        [x, k2, cot],
        [
            pltpu.VMEM((2048, 256), BF),
            pltpu.VMEM((27, 8, 64), BF),
            pltpu.VMEM((512, 64), BF),
            pltpu.VMEM((2, 1056, 128), F32),
            pltpu.VMEM((128, 1280), F32),
            pltpu.VMEM((576, 128), F32),
            pltpu.SemaphoreType.DMA((3,)),
        ],
        space=pl.ANY,
        limit=60 * 1024 * 1024,
    )
    plane = move(plane, "dev", 1)
    row = move(row, "ha", 1)
    n_dev, n_ha = lax.axis_size("dev"), lax.axis_size("ha")
    corner = lax.ppermute(
        corner,
        ("dev", "ha"),
        [(d * n_ha + h, (d + 1) * n_ha + h + 1) for d in range(n_dev - 1) for h in range(n_ha - 1)],
    )
    a2 = exchange(packed, "ha")
    own, wt = call(
        turn_image_body,
        [shape((64, 96, 128), BF), shape((64, 864), BF)],
        [x, k1],
        [pltpu.VMEM((2112, 128), F32), pltpu.VMEM((2112, 128), F32)],
        flops=300000000,
    )
    slope, pooled, low, top = call(
        first_layer_body,
        [
            shape((64, 2048), F32),
            shape((64, 256), BF),
            shape((16, 96, 128), BF),
            shape((5, 96, 128), BF),
        ],
        [own, wt, plane, row, corner],
        [pltpu.VMEM((672, 128), F32), pltpu.VMEM((672, 128), F32)],
        flops=400000000,
    )
    other = swap(pooled, "dev", 0)
    (rims,) = call(rims_body, [shape((128, 128), BF)], [pooled, other])
    route = []
    for d in range(n_dev):
        for h in range(d % 2, n_ha - 1, 2):
            route += [(d * n_ha + h, d * n_ha + h + 1), (d * n_ha + h + 1, d * n_ha + h)]
    rims = lax.ppermute(rims, ("dev", "ha"), route)
    a2_other = swap(a2, "dev", 0)
    w2, wb = call(turn_filters_body, [shape((128, 1792), BF), shape((64, 3456), BF)], [a2, a2_other])
    cot_cross = swap(a2[:, 896:1280], "dev", 1)
    rims_core, cot_cross = lax.optimization_barrier((swap(rims, "dev", 0), cot_cross))
    (pair,) = call(widen_body, [shape((128, 512), BF)], [pooled, other, rims, rims_core])
    cross = swap(pair, "dev", 1)
    patches, act, delta = call(
        second_layer_body,
        [shape((2944, 384), BF), shape((128, 256), BF), shape((384, 384), BF)],
        [pair, cross, swap(cross, "dev", 0), w2, a2, a2_other, cot_cross],
        flops=500000000,
    )
    keep_two, give_two = call(
        grad_two_body, [shape((128, 896), F32), shape((128, 896), BF)], [delta, patches], flops=180000000
    )
    grad_pooled, keep_one, give_one = call(
        backward_body,
        [shape((64, 4, 64), BF), shape((128, 256), F32), shape((128, 256), BF)],
        [delta, wb, slope, own, low, top],
        [pltpu.VMEM((3456, 256), BF), pltpu.VMEM((2, 272, 128), F32)],
        flops=400000000,
    )
    (first,) = call(
        sum_chip_body,
        [shape((128, 1152), BF)],
        [keep_two, swap(give_two, "dev", 0), keep_one, swap(give_one, "dev", 0)],
    )
    same_core = [list(range(core, lax.axis_size("dev"), 2)) for core in range(2)]
    (second,) = call(
        sum_depth_body,
        [shape((896, 128), BF)],
        [exchange(first, "dev", same_core), act],
        [pltpu.VMEM((960, 128), F32)],
    )
    second = exchange(second, "ha")
    (third,) = call(sum_height_body, [shape((320, 128), BF)], [second])
    (activation,) = call(lay_activation_body, [shape((512, 64), BF)], [second], [pltpu.VMEM((576, 128), F32)])
    third = exchange(third, "dev", same_core)
    one, two = call(
        finish_body,
        [shape((27, 32, 64), F32), shape((27, 8, 64), F32)],
        [third, swap(third, "dev", 0)],
        [pltpu.VMEM((3, 288, 128), F32)],
    )
    grad_one = jnp.transpose(one.reshape(3, 3, 3, 32, 64), (4, 3, 0, 1, 2))
    grad_two = jnp.transpose(two.reshape(3, 3, 3, 8, 64), (3, 4, 0, 1, 2))
    return (activation.reshape(8, 1, 64, 64), grad_pooled.reshape(64, 1, 4, 64), grad_one, grad_two)


def solution(mesh):
    return jax.shard_map(
        shards,
        mesh=mesh,
        in_specs=(
            P(None, "dev", "ha", None),
            P(),
            P("ha", None, None, None, None),
            P("ha", "dev", None, None),
        ),
        out_specs=(
            P("ha", "dev", None, None),
            P(None, "dev", "ha", None),
            P(),
            P("ha", None, None, None, None),
        ),
        check_vma=False,
    )
```
